32 devices in a mesh: ctx: 16 (over z, y, core), ws: 2 (over x).
Axes of the slice: x: 2, y: 2, z: 4, core: 2. Of those that a mesh axis runs over, the one named last changes fastest.
Arguments:
- layer_input: bfloat16 [16, 2, 128, 2048], P('ctx', 'ws'), may hold values from -6 to 6
- out_grad: bfloat16 [16, 2, 128, 2048], P('ctx', 'ws'), may hold values from -6 to 6
- seq_lengths: int32 [2], replicated, may hold values from 512 to 2048, as said below
- block_deal: int32 [32], replicated, may hold values from 0 to 31, as said below
- expert_routes: int32 [16, 2, 128, 8], P('ctx', 'ws'), may hold values from 0 to 15, all different within a row; in each aligned block of 128 rows (0 to 127, 128 to 255, ..., all dimensions but the last counted through in order) at most 80 rows name the same one
- attn_gain: float32 [2048], replicated, may hold values from 0.5 to 1.5
- query_gain: float32 [2048], replicated, may hold values from 0.5 to 1.5
- key_gain: float32 [2048], replicated, may hold values from 0.5 to 1.5
- ffn_gain: float32 [2048], replicated, may hold values from 0.5 to 1.5
- w_query: float32 [2048, 2048], P(('ctx', 'ws')), may hold values from -0.125 to 0.125
- w_key: float32 [2048, 2048], P(('ctx', 'ws')), may hold values from -0.125 to 0.125
- w_value: float32 [2048, 2048], P(('ctx', 'ws')), may hold values from -0.125 to 0.125
- w_out: float32 [2048, 2048], P(('ctx', 'ws')), may hold values from -0.75 to 0.75
- w_router: float32 [2048, 16], P(('ctx', 'ws')), may hold values from -0.0625 to 0.0625
- w_gate: float32 [16, 2048, 1024], P('ctx', 'ws'), may hold values from -0.125 to 0.125
- w_up: float32 [16, 2048, 1024], P('ctx', 'ws'), may hold values from -0.125 to 0.125
- w_down: float32 [16, 1024, 2048], P('ctx', 'ws'), may hold values from -12 to 12
Outputs:
- layer_out: bfloat16 [16, 2, 128, 2048], P('ctx', 'ws')
- grad_input: float32 [16, 2, 128, 2048], P('ctx', 'ws')
- grad_attn_gain: float32 [2048], P(('ctx', 'ws'))
- grad_query_gain: float32 [2048], P(('ctx', 'ws'))
- grad_key_gain: float32 [2048], P(('ctx', 'ws'))
- grad_ffn_gain: float32 [2048], P(('ctx', 'ws'))
- grad_w_query: float32 [2048, 2048], P(('ctx', 'ws'))
- grad_w_key: float32 [2048, 2048], P(('ctx', 'ws'))
- grad_w_value: float32 [2048, 2048], P(('ctx', 'ws'))
- grad_w_out: float32 [2048, 2048], P(('ctx', 'ws'))
- grad_w_router: float32 [2048, 16], P(('ctx', 'ws'))
- grad_w_gate: float32 [16, 2048, 1024], P('ctx', 'ws')
- grad_w_up: float32 [16, 2048, 1024], P('ctx', 'ws')
- grad_w_down: float32 [16, 1024, 2048], P('ctx', 'ws')
The draws below stay inside these ranges and needn't reach their ends.
Inputs may be any that keep to these rules, and one draw needn't show every extreme that they name: `seq_lengths`: one slot, which one drawn from the seed, is live over all 2048 positions; the other over at least 512. `block_deal`: each block number appears once; entries 2 k and 2 k + 1 sum to 31. `expert_routes`: each token names 8 different experts. Of the 128 tokens of one device, at most 80 name any one expert, and on some device one expert is named by exactly 80.
All inputs are finite; a program needn't handle non-finite values.
Results may differ from the reference program's by a relative error of at most 0.02.
Values may be sent and summed in bfloat16 or wider, within the bound.
No kernel may reach another device: no remote copies, remote signals or barrier semaphores. Data moves between devices by JAX's collectives and lax.ppermute only.
A program may use at most 896 MiB of HBM per device.

```python
import math
import jax
import jax.numpy as jnp
import numpy as np
from jax import lax

D = 2048
HEADS = 16
HD = 128
FF = 1024
TOP = 8
SLOTS = 2
HB = 32
EXPERTS = 16
TOK_DEV = 128
BLK = 64
SEQ = 2048
CAP = 80
QBLOCK = 512
N_CTX = 16
N_WS = 2
DEVICES = 32


def draw_seq_lengths(key, part):
    key = jax.random.fold_in(key, 11)
    full_key, other_key = jax.random.split(key)
    full_slot = jax.random.randint(full_key, (), 0, SLOTS)
    other_len = jax.random.randint(other_key, (SLOTS,), SEQ // 4, SEQ + 1)
    return jnp.where(jnp.arange(SLOTS) == full_slot, SEQ, other_len).astype(jnp.int32)


def draw_block_deal(key, part):
    key = jax.random.fold_in(key, 23)
    pair_key, flip_key = jax.random.split(key)
    pair_order = jax.random.permutation(pair_key, N_CTX)
    flip_bits = jax.random.randint(flip_key, (N_CTX,), 0, 2)
    high_end = 2 * N_CTX - 1 - pair_order
    first_block = jnp.where(flip_bits == 1, high_end, pair_order)
    second = jnp.where(flip_bits == 1, pair_order, high_end)
    return jnp.stack([first_block, second], axis=1).reshape(2 * N_CTX).astype(jnp.int32)


def block_scale(stream_key, shape, cuts, low, high):
    def one(dim, blocks):
        steps = jax.random.uniform(jax.random.fold_in(jax.random.fold_in(stream_key, 6), dim), (blocks,), jnp.float32, low / len(cuts), high / len(cuts))
        return jnp.repeat(jnp.exp(steps), shape[dim] // blocks).reshape((-1,) + (1,) * (len(shape) - dim - 1))

    loudness = one(*cuts[0])
    for cut in cuts[1:]:
        loudness = loudness * one(*cut)
    return loudness


def deal_out(own_key, own, number, rows, amount, top, reach, slope):
    order = jax.random.permutation(own_key, amount)
    crowded, common = load_shares(amount, rows * top, reach, slope, True), load_shares(amount, rows * top, reach, slope, False)
    places = jnp.arange(amount)

    def named(sizes, offset_by):
        used = int((sizes > 0).sum())
        fixed = max(1, used // 4)
        moved = fixed + (places - fixed + offset_by * (used - fixed)) % max(1, amount - fixed)
        return jnp.zeros((amount,), jnp.int32).at[order[jnp.where(places < fixed, places, moved)]].set(jnp.asarray(sizes, jnp.int32))

    sizes = jnp.where(number % 4 == 0, named(crowded, number // 4), named(common, number - number // 4 - 1))
    mixed = jax.random.permutation(jax.random.fold_in(own, 3), amount)
    donor, sink = mixed[0:amount // 2 * 2:2], mixed[1:amount // 2 * 2:2]
    margin = jnp.minimum(sizes[donor] - 1, reach - sizes[sink]) // 2
    margin = jnp.where((donor == order[0]) | (sink == order[0]) | (sizes[sink] == 0), 0, jnp.maximum(margin, 0))
    moved = jax.random.randint(jax.random.fold_in(own, 4), (amount // 2,), 0, 1 << 20) % (margin + 1)
    sizes = sizes.at[donor].add(-moved).at[sink].add(moved)
    labels = jnp.searchsorted(jnp.cumsum(sizes), jnp.arange(rows * top), side="right").astype(jnp.int32)
    grid = labels.reshape(top, rows).T
    grid = grid[jax.random.permutation(jax.random.fold_in(own, 1), rows)]
    offset_by = jax.random.randint(jax.random.fold_in(own, 2), (rows, 1), 0, top)
    return jnp.take_along_axis(grid, (jnp.arange(top)[None, :] + offset_by) % top, axis=1)


def load_shares(count, total, reach, skew, full):
    portions = [(1 << 20) // math.isqrt(standing ** skew) + 1 for standing in range(1, count + 1)]
    largest = reach if full else min(reach, max(-(-total // count), total * portions[0] // sum(portions)))
    least = 1 if total - largest >= count - 1 else 0
    counts, rest = [largest] + [least] * (count - 1), total - largest - least * (count - 1)
    while rest > 0:
        candidates = [i for i in range(1, count) if counts[i] < largest] or [i for i in range(1, count) if counts[i] < reach]
        whole, left = sum([portions[i] for i in candidates]), rest
        for i in candidates:
            extra = min(reach - counts[i], max(1, left * portions[i] // whole), rest)
            counts[i] = counts[i] + extra
            rest = rest - extra
    return np.array(counts)


def scatter_about(stream_key, shape, deviation, most, cuts=(), held_as=jnp.bfloat16):
    gain = block_scale(stream_key, shape, cuts, -0.22, 0.18) if cuts else 1.0
    values = jax.random.normal(stream_key, shape, jnp.float32) * deviation * gain
    return jnp.minimum(jnp.maximum(values, -most), most).astype(held_as)


def setup_inputs(seed: int = 0) -> dict:
    streams_of = jax.random.split(jax.random.key(seed), 18)
    layer_input = scatter_about(streams_of[0], (N_CTX, N_WS, TOK_DEV, D), 1.0, 6.0, ((0, 16), (1, 2)))
    out_grad = scatter_about(streams_of[1], (N_CTX, N_WS, TOK_DEV, D), 1.0, 6.0, ((0, 16), (1, 2)))
    seq_lengths = draw_seq_lengths(jax.random.fold_in(streams_of[17], 71), 0)
    block_deal = draw_block_deal(jax.random.fold_in(streams_of[17], 71), 0)
    expert_routes_keys = jax.random.split(jax.random.fold_in(streams_of[4], 1), N_CTX * N_WS * TOK_DEV // TOK_DEV)
    expert_routes_turns = jax.random.permutation(jax.random.fold_in(streams_of[4], 3), N_CTX * N_WS * TOK_DEV // TOK_DEV)
    expert_routes = jax.vmap(lambda own, number: deal_out(jax.random.fold_in(streams_of[4], 2), own, number, TOK_DEV, EXPERTS, TOP, CAP, 1))(expert_routes_keys, expert_routes_turns).reshape((N_CTX, N_WS, TOK_DEV, TOP))
    attn_gain = jnp.clip(1.0 + 0.1 * jax.random.normal(streams_of[5], (D,), jnp.float32), 0.5, 1.5)
    query_gain = jnp.clip(1.0 + 0.1 * jax.random.normal(streams_of[6], (D,), jnp.float32), 0.5, 1.5)
    key_gain = jnp.clip(1.0 + 0.1 * jax.random.normal(streams_of[7], (D,), jnp.float32), 0.5, 1.5)
    ffn_gain = jnp.clip(1.0 + 0.1 * jax.random.normal(streams_of[8], (D,), jnp.float32), 0.5, 1.5)
    w_query = scatter_about(streams_of[9], (D, D), D ** -0.5, 0.125, ((0, 32),), jnp.float32)
    w_key = scatter_about(streams_of[10], (D, D), D ** -0.5, 0.125, ((0, 32),), jnp.float32)
    w_value = scatter_about(streams_of[11], (D, D), D ** -0.5, 0.125, ((0, 32),), jnp.float32)
    w_out = scatter_about(streams_of[12], (D, D), (max(1, D // 32)) ** -0.5, 0.75, ((0, 32),), jnp.float32)
    w_router = scatter_about(streams_of[13], (D, EXPERTS), (4 * D) ** -0.5, 0.0625, ((0, 32),), jnp.float32)
    w_gate = scatter_about(streams_of[14], (EXPERTS, D, FF), D ** -0.5, 0.125, ((0, 16), (1, 2)), jnp.float32)
    w_up = scatter_about(streams_of[15], (EXPERTS, D, FF), D ** -0.5, 0.125, ((0, 16), (1, 2)), jnp.float32)
    w_down = scatter_about(streams_of[16], (EXPERTS, FF, D), 2.0, 12.0, ((0, 16), (1, 2)), jnp.float32)
    return dict(layer_input=layer_input, out_grad=out_grad, seq_lengths=seq_lengths, block_deal=block_deal, expert_routes=expert_routes, attn_gain=attn_gain, query_gain=query_gain, key_gain=key_gain, ffn_gain=ffn_gain, w_query=w_query, w_key=w_key, w_value=w_value, w_out=w_out, w_router=w_router, w_gate=w_gate, w_up=w_up, w_down=w_down)


NORM_EPS = 1e-05
ROPE_BASE = 10000.0
MASK_FLOOR = -1e+30
PRECISE = lax.Precision.HIGHEST

@jax.custom_vjp
def low(v):
    return lax.optimization_barrier(v.astype(jnp.bfloat16)).astype(jnp.float32)

@jax.custom_vjp
def low_back(v):
    return v

def low_keep(v):
    return (low(v), None)

def low_pass(kept, grad):
    return (grad,)

def back_keep(v):
    return (v, None)

def back_low(kept, grad):
    return (low(grad),)
low.defvjp(low_keep, low_pass)
low_back.defvjp(back_keep, back_low)

def rms_norm(field, norm_gain):
    return field * lax.rsqrt(lax.optimization_barrier(jnp.mean(field * field, axis=-1, keepdims=True)) + NORM_EPS) * norm_gain

def rotate(field, positions):
    row_count = field.shape[0]
    head_count = field.shape[1] // HD
    half_dim = HD // 2
    shaped = field.reshape(row_count, head_count, HD)
    inv_freq = jnp.exp(jnp.arange(half_dim, dtype=jnp.float32) * (-2.0 * math.log(ROPE_BASE) / HD))
    angles = positions.astype(jnp.float32)[:, None] * inv_freq[None, :]
    cosine = jnp.cos(angles)[:, None, :]
    sine_part = jnp.sin(angles)[:, None, :]
    lead_half = shaped[..., :half_dim]
    tail_half = shaped[..., half_dim:]
    turned = jnp.concatenate([lead_half * cosine - tail_half * sine_part, tail_half * cosine + lead_half * sine_part], axis=-1)
    return turned.reshape(row_count, head_count * HD)

def token_places(block_deal):
    flat_index = jnp.arange(DEVICES * TOK_DEV, dtype=jnp.int32)
    device = flat_index // TOK_DEV
    local_row = flat_index % TOK_DEV
    ctx_pos = device // N_WS
    ws_pos = device % N_WS
    slot_of = local_row // (2 * HB)
    block_pick = local_row // HB % 2
    row_in = local_row % HB
    positions = block_deal[2 * ctx_pos + block_pick] * BLK + ws_pos * HB + row_in
    return (positions.astype(jnp.int32), slot_of.astype(jnp.int32))

def route_tables(expert_routes):
    per_device = expert_routes.reshape(DEVICES, TOK_DEV * TOP)
    hot_rows = (per_device[:, :, None] == jnp.arange(EXPERTS, dtype=jnp.int32)[None, None, :]).astype(jnp.int32)
    slot_rank = lax.optimization_barrier(jnp.sum((jnp.cumsum(hot_rows, axis=1) - 1) * hot_rows, axis=2))
    device_ids = jnp.arange(DEVICES, dtype=jnp.int32)[:, None]
    target = (per_device * (DEVICES * CAP) + device_ids * CAP + slot_rank).astype(jnp.int32)
    copies = DEVICES * TOK_DEV * TOP
    source = jnp.full((EXPERTS * DEVICES * CAP,), copies, jnp.int32).at[target.reshape(copies)].set(jnp.arange(copies, dtype=jnp.int32))
    return (target.reshape(DEVICES * TOK_DEV, TOP), source)

def attend_slot(q_heads, k_heads, v_heads, positions, live_key):
    block_count = SEQ // QBLOCK

    def one_block(block_args):
        q_block, pos_block = block_args
        raw_score = jnp.einsum('qhd,khd->hqk', q_block, k_heads, precision=PRECISE) * HD ** (-0.5)
        raw_score = low_back(raw_score)
        visible = (positions[None, :] <= pos_block[:, None]) & live_key[None, :]
        scores = jnp.where(visible[None], raw_score, MASK_FLOOR)
        row_max = lax.optimization_barrier(jnp.max(scores, axis=-1, keepdims=True))
        expo_vals = jnp.exp(scores - row_max)
        prob_low = low(expo_vals / lax.optimization_barrier(jnp.sum(expo_vals, axis=-1, keepdims=True)))
        return jnp.einsum('hqk,khd->qhd', prob_low, v_heads, precision=PRECISE)
    outputs = lax.map(jax.checkpoint(one_block), (q_heads.reshape(block_count, QBLOCK, HEADS, HD), positions.reshape(block_count, QBLOCK)))
    return outputs.reshape(SEQ, HEADS * HD)

def reference(layer_input, out_grad, seq_lengths, block_deal, expert_routes, attn_gain, query_gain, key_gain, ffn_gain, w_query, w_key, w_value, w_out, w_router, w_gate, w_up, w_down):
    total_rows = DEVICES * TOK_DEV
    positions, slot_of = token_places(block_deal)
    live_rows = positions < seq_lengths[slot_of]
    target, source = route_tables(expert_routes)
    route_flat = expert_routes.reshape(total_rows, TOP)
    pos_slots = positions.reshape(DEVICES, SLOTS, 2 * HB)
    live_slots = live_rows.reshape(DEVICES, SLOTS, 2 * HB)

    def by_slot(field, slot_id):
        return field.reshape(DEVICES, SLOTS, 2 * HB, HEADS, HD)[:, slot_id].reshape(SEQ, HEADS, HD)

    def forward(input_f, gain_attn, gain_query, gain_key, gain_ffn, wq_f, wk_f, wv_f, wo_f, wr_f, wg_f, wu_f, wd_f):
        attn_in = low(rms_norm(input_f, gain_attn))
        q_pre = low_back(jnp.dot(attn_in, low(wq_f), precision=PRECISE))
        k_pre = low_back(jnp.dot(attn_in, low(wk_f), precision=PRECISE))
        v_low = low_back(low(jnp.dot(attn_in, low(wv_f), precision=PRECISE)))
        q_rot = low_back(low(rotate(rms_norm(q_pre, gain_query), positions)))
        k_rot = low_back(low(rotate(rms_norm(k_pre, gain_key), positions)))
        slot_outs = []
        for slot_id in range(SLOTS):
            slot_attn = attend_slot(by_slot(q_rot, slot_id), by_slot(k_rot, slot_id), by_slot(v_low, slot_id), pos_slots[:, slot_id].reshape(SEQ), live_slots[:, slot_id].reshape(SEQ))
            slot_outs.append(slot_attn.reshape(DEVICES, 1, 2 * HB, D))
        attn_low = low_back(low(jnp.concatenate(slot_outs, axis=1).reshape(total_rows, D)))
        resid_mid = input_f + low_back(jnp.dot(attn_low, low(wo_f), precision=PRECISE))
        ffn_in = low(rms_norm(resid_mid, gain_ffn))
        logits = low_back(jnp.dot(ffn_in, low(wr_f), precision=PRECISE))
        router_prob = jax.nn.softmax(logits, axis=-1)
        gate_vals = jnp.take_along_axis(router_prob, route_flat, axis=1)
        padded_in = jnp.concatenate([ffn_in, jnp.zeros((1, D), jnp.float32)], axis=0)

        def expert(expert_args):
            row_ids, gate_w, up_w, down_w = expert_args
            routed = low_back(padded_in[row_ids])
            gate_pre = low_back(jnp.dot(routed, low(gate_w), precision=PRECISE))
            up_pre = low_back(jnp.dot(routed, low(up_w), precision=PRECISE))
            hidden_low = low(jax.nn.silu(gate_pre) * up_pre)
            return low_back(low(jnp.dot(hidden_low, low(down_w), precision=PRECISE)))
        row_table = (source // TOP).reshape(EXPERTS, DEVICES * CAP)
        returned = lax.map(jax.checkpoint(expert), (row_table, wg_f, wu_f, wd_f))
        copy_out = returned.reshape(EXPERTS * DEVICES * CAP, D)[target]
        mixture = lax.optimization_barrier(jnp.sum(gate_vals[:, :, None] * copy_out, axis=1))
        return resid_mid + mixture
    primals = (layer_input.reshape(total_rows, D).astype(jnp.float32), attn_gain, query_gain, key_gain, ffn_gain, w_query, w_key, w_value, w_out, w_router, w_gate, w_up, w_down)
    result, pull_back = jax.vjp(forward, *primals)
    masked_grad = out_grad.reshape(total_rows, D).astype(jnp.float32) * live_rows[:, None].astype(jnp.float32)
    grads = pull_back(masked_grad)
    return (result.astype(jnp.bfloat16).reshape(layer_input.shape), grads[0].reshape(layer_input.shape), grads[1], grads[2], grads[3], grads[4], grads[5], grads[6], grads[7], grads[8], grads[9], grads[10], grads[11], grads[12])
```

```python
import math

import jax
import jax.numpy as jnp
from jax import lax
from jax.sharding import PartitionSpec as P

HD = 128
SLOTS = 2

NORM_EPS = 1e-05
ROPE_BASE = 10000.0
MASK_FLOOR = -1e30

LOW = jnp.bfloat16
HIGH = jnp.float32


def dot(left, right, dims=((1,), (0,))):
    return lax.dot_general(left, right, (dims, ((), ())), preferred_element_type=HIGH)


def inv_rms(field):
    return lax.rsqrt(jnp.mean(field * field, axis=-1, keepdims=True) + NORM_EPS)


def rms_back(field, scale, d_hat):
    hat = field * scale
    return scale * (d_hat - hat * jnp.mean(d_hat * hat, axis=-1, keepdims=True))


def rope_tables(positions):
    half_dim = HD // 2
    inv_freq = jnp.exp(jnp.arange(half_dim, dtype=HIGH) * (-2.0 * math.log(ROPE_BASE) / HD))
    angles = positions.astype(HIGH)[:, None] * inv_freq[None, :]
    return jnp.cos(angles), jnp.sin(angles)


def rotate(field, cosine, sine):
    lead, tail = field[:, : HD // 2], field[:, HD // 2 :]
    return jnp.concatenate([lead * cosine - tail * sine, tail * cosine + lead * sine], axis=1)


def swap_ws(field):
    mine = lax.axis_index("ws")
    count = lax.axis_size("ws")
    if count != 2:
        return lax.all_to_all(field, "ws", 0, 0, tiled=True)
    own = lax.dynamic_index_in_dim(field, mine, 0, keepdims=False)
    away = lax.dynamic_index_in_dim(field, 1 - mine, 0, keepdims=False)
    came = lax.ppermute(away, "ws", [(0, 1), (1, 0)])
    first = mine == 0
    return jnp.stack([jnp.where(first, own, came), jnp.where(first, came, own)], axis=0)


def sum_ctx(field):
    count = lax.axis_size("ctx")
    if count & (count - 1):
        return lax.psum(field, "ctx")
    step = 1
    while step < count:
        field = field + lax.ppermute(field, "ctx", [(i, i ^ step) for i in range(count)])
        step *= 2
    return field


def gather_ctx(block):
    return lax.all_gather(block, "ctx", axis=0, tiled=True)


def scatter_ctx(field):
    return lax.psum_scatter(field, "ctx", scatter_dimension=0, tiled=True)


def local(
    layer_input,
    out_grad,
    seq_lengths,
    block_deal,
    expert_routes,
    attn_gain,
    query_gain,
    key_gain,
    ffn_gain,
    w_query,
    w_key,
    w_value,
    w_out,
    w_router,
    w_gate,
    w_up,
    w_down,
):
    ws_count = lax.axis_size("ws")
    ctx_count = lax.axis_size("ctx")
    c = lax.axis_index("ctx")
    w = lax.axis_index("ws")
    tokens, width = layer_input.shape[2:]
    heads = width // HD
    parts = ctx_count // heads
    head = c // parts
    part = c % parts
    own_part = c // heads
    slot_rows = tokens // SLOTS
    half_block = slot_rows // 2
    rows = w_query.shape[0]
    experts = w_router.shape[1]
    span = ctx_count * tokens
    part_span = span // parts

    starts = block_deal.reshape(ctx_count, 1, 2, 1) * (half_block * ws_count)
    in_block = jnp.arange(half_block, dtype=jnp.int32)
    pair_pos = starts + (
        jnp.arange(ws_count, dtype=jnp.int32)[None, :, None, None] * half_block + in_block
    )
    pos_slot = pair_pos.reshape(span)
    live_slot = pos_slot < seq_lengths[w]
    own_pos = lax.dynamic_index_in_dim(
        (starts + w * half_block + in_block)[:, 0], c, 0, keepdims=False
    ).reshape(1, slot_rows)
    live_own = (own_pos < seq_lengths[:, None]).reshape(tokens, 1)

    x = layer_input.reshape(tokens, width).astype(HIGH)
    x_scale = inv_rms(x)
    attn_in = (x * x_scale * attn_gain).astype(LOW)
    slot_in = gather_ctx(swap_ws(attn_in.reshape(SLOTS, slot_rows, width)).reshape(tokens, width))

    own_qkv = jnp.stack([w_query, w_key, w_value]).astype(LOW)
    by_head = own_qkv.reshape(3, rows, heads, HD).transpose(2, 1, 0, 3).reshape(heads, rows, 3 * HD)
    if parts > 1:
        by_head = jnp.repeat(by_head, parts, axis=0)
    head_rows = lax.all_to_all(by_head, "ctx", 0, 0, tiled=True)
    head_rows = lax.all_gather(head_rows, "ws", axis=1)
    w_head = head_rows.reshape(width, 3 * HD)

    o_weight = lax.all_gather(w_out.astype(LOW), ("ctx", "ws"), axis=0, tiled=True)
    r_weight = lax.all_gather(w_router.astype(LOW), ("ctx", "ws"), axis=0, tiled=True)
    g_weight = lax.all_gather(w_gate[0].astype(LOW), "ws", axis=0, tiled=True)
    u_weight = lax.all_gather(w_up[0].astype(LOW), "ws", axis=0, tiled=True)
    d_weight = lax.all_gather(w_down[0].astype(LOW), "ws", axis=0, tiled=True)
    grad_own = jnp.where(live_own, out_grad.reshape(tokens, width), 0).astype(LOW)
    grad_plane = gather_ctx(grad_own)
    routes = lax.all_gather(expert_routes.reshape(tokens, -1), "ctx", axis=0, tiled=True)

    qkv = dot(slot_in, w_head)
    q_pre, k_pre = qkv[:, :HD], qkv[:, HD : 2 * HD]
    v_low = qkv[:, 2 * HD :].astype(LOW)
    squares = sum_ctx(jnp.stack([jnp.sum(q_pre * q_pre, axis=1), jnp.sum(k_pre * k_pre, axis=1)]))
    qk_scale = lax.rsqrt(squares * (1.0 / (parts * width)) + NORM_EPS)
    q_hat = q_pre * qk_scale[0][:, None]
    k_hat = k_pre * qk_scale[1][:, None]
    q_gain = lax.dynamic_slice_in_dim(query_gain, head * HD, HD, 0)
    k_gain = lax.dynamic_slice_in_dim(key_gain, head * HD, HD, 0)
    cosine, sine = rope_tables(pos_slot)
    q_low = rotate(q_hat * q_gain, cosine, sine).astype(LOW)
    k_low = rotate(k_hat * k_gain, cosine, sine).astype(LOW)

    def of_part(field):
        if parts == 1:
            return field
        return lax.dynamic_slice_in_dim(field, part * part_span, part_span, 0)

    q_part = of_part(q_low)
    pos_query = of_part(pos_slot)
    score_scale = HD ** (-0.5)
    visible = (pos_slot[None, :] <= pos_query[:, None]) & live_slot[None, :]
    scores = jnp.where(visible, dot(q_part, k_low, ((1,), (1,))) * score_scale, MASK_FLOOR)
    row_max = jnp.max(scores, axis=1, keepdims=True)
    expo = jnp.exp(scores - row_max)
    row_sum = jnp.sum(expo, axis=1, keepdims=True)
    attn_head = dot((expo / row_sum).astype(LOW), v_low)
    log_total = row_max + jnp.log(row_sum)
    attn_head_low = attn_head.astype(LOW)

    out_chunks = attn_head_low.reshape(heads, tokens, HD)
    if parts > 1:
        out_chunks = lax.dynamic_update_slice_in_dim(
            jnp.zeros((ctx_count, tokens, HD), LOW), out_chunks, part * heads, 0
        )
    came = lax.all_to_all(out_chunks, "ctx", 0, 0, tiled=True)
    if parts > 1:
        came = lax.dynamic_index_in_dim(
            came.reshape(heads, parts, tokens, HD), own_part, 1, keepdims=False
        )
    attn_rows = came.transpose(1, 0, 2).reshape(ws_count, slot_rows, width)
    attn_low = swap_ws(attn_rows).reshape(tokens, width)

    mid = x + dot(attn_low, o_weight)
    mid_scale = inv_rms(mid)
    ffn_in = (mid * mid_scale * ffn_gain).astype(LOW)
    plane_in = gather_ctx(ffn_in)

    router_prob = jax.nn.softmax(dot(plane_in, r_weight), axis=-1)
    prob_own = lax.dynamic_slice_in_dim(router_prob, c, 1, 1)
    routed = jnp.any(routes == c, axis=1, keepdims=True)
    gate = jnp.where(routed, prob_own, 0.0)
    d_hidden_raw = dot(grad_plane, d_weight, ((1,), (1,)))
    gate_pre = dot(plane_in, g_weight)
    up_pre = dot(plane_in, u_weight)
    sigma = jax.nn.sigmoid(gate_pre)
    act = gate_pre * sigma
    hidden = (act * up_pre).astype(LOW)
    d_gate = jnp.where(
        routed, jnp.sum(hidden.astype(HIGH) * d_hidden_raw, axis=1, keepdims=True), 0.0
    )
    prob_sum = sum_ctx((prob_own * d_gate).reshape(-1, 128)).reshape(-1, 1)
    d_log = (prob_own * (d_gate - prob_sum)).astype(LOW)
    d_hidden = gate * d_hidden_raw
    d_gate_low = (d_hidden * up_pre * (sigma * (1.0 + gate_pre * (1.0 - sigma)))).astype(LOW)
    d_up_low = (d_hidden * act).astype(LOW)
    r_column = lax.dynamic_slice_in_dim(r_weight, c, 1, 1).reshape(1, width)
    d_copy = (
        dot(d_gate_low, g_weight, ((1,), (1,)))
        + dot(d_up_low, u_weight, ((1,), (1,)))
        + d_log.astype(HIGH) * r_column.astype(HIGH)
    ).astype(LOW)
    d_ffn = scatter_ctx(d_copy).astype(HIGH)

    produced = dot(hidden, d_weight).astype(LOW).astype(HIGH)
    mixture = scatter_ctx((gate * produced).astype(LOW)).astype(HIGH)
    layer_out = (mid + mixture).astype(LOW)

    hidden_gated = (gate * hidden.astype(HIGH)).astype(LOW)

    def expert_grad(left, right):
        total = dot(left, right, ((0,), (0,)))
        return lax.psum_scatter(
            total.astype(LOW), "ws", scatter_dimension=0, tiled=True
        ).astype(HIGH)[None]

    grad_w_down = expert_grad(hidden_gated, grad_plane)
    grad_w_gate = expert_grad(plane_in, d_gate_low)
    grad_w_up = expert_grad(plane_in, d_up_low)
    router_column = jnp.sum(plane_in.astype(HIGH) * d_log.astype(HIGH), axis=0)

    mid_hat = mid * mid_scale
    ffn_gain_part = jnp.sum(d_ffn * mid_hat, axis=0)
    d_mid = grad_own.astype(HIGH) + rms_back(mid, mid_scale, d_ffn * ffn_gain)
    d_mid_low = d_mid.astype(LOW)

    small = lax.all_gather(jnp.stack([ffn_gain_part, router_column]), ("ctx", "ws"), axis=0)
    small = lax.dynamic_slice_in_dim(small, (c * ws_count + w) * rows, rows, 2)
    grad_ffn_gain = jnp.sum(small[:, 0], axis=0)
    grad_w_router = jnp.sum(small[:, 1].reshape(experts, ws_count, rows), axis=1).T

    d_attn = dot(d_mid_low, o_weight, ((1,), (1,))).astype(LOW)
    d_attn_rows = swap_ws(d_attn.reshape(SLOTS, slot_rows, width)).reshape(tokens, heads, HD)
    in_chunks = d_attn_rows.transpose(1, 0, 2)
    if parts > 1:
        in_chunks = lax.dynamic_update_slice(
            jnp.zeros((heads, parts, tokens, HD), LOW), in_chunks[:, None], (0, own_part, 0, 0)
        ).reshape(ctx_count, tokens, HD)
    d_attn_head = lax.all_to_all(in_chunks, "ctx", 0, 0, tiled=True)
    if parts > 1:
        d_attn_head = lax.dynamic_slice_in_dim(d_attn_head, part * heads, heads, 0)
    d_attn_head = d_attn_head.reshape(part_span, HD)

    slot_d_mid = gather_ctx(
        swap_ws(d_mid_low.reshape(SLOTS, slot_rows, width)).reshape(tokens, width)
    )
    out_rows = dot(attn_head_low, of_part(slot_d_mid), ((0,), (0,)))
    if parts > 1:
        groups = [[h * parts + i for i in range(parts)] for h in range(heads)]
        out_rows = lax.psum_scatter(
            out_rows, "ctx", scatter_dimension=0, axis_index_groups=groups, tiled=True
        )
    grad_w_out = jnp.sum(swap_ws(out_rows.reshape(ws_count, rows, width)), axis=0)

    delta = jnp.sum(d_attn_head.astype(HIGH) * attn_head, axis=1, keepdims=True)
    prob = jnp.exp(
        jnp.where(visible, dot(q_part, k_low, ((1,), (1,))) * score_scale, MASK_FLOOR) - log_total
    )
    d_prob = dot(d_attn_head, v_low, ((1,), (1,)))
    d_score = (prob * (d_prob - delta)).astype(LOW)
    d_q_part = (dot(d_score, k_low) * score_scale).astype(LOW)
    d_k_rot = (dot(d_score, q_part, ((0,), (0,))) * score_scale).astype(LOW)
    d_v_low = dot(prob.astype(LOW), d_attn_head, ((0,), (0,))).astype(LOW)
    d_q_rot = d_q_part
    if parts > 1:
        d_q_rot = lax.dynamic_update_slice_in_dim(
            jnp.zeros((span, HD), LOW), d_q_part, part * part_span, 0
        )
    d_q_norm = rotate(d_q_rot.astype(HIGH), cosine, -sine)
    d_k_norm = rotate(d_k_rot.astype(HIGH), cosine, -sine)
    gain_parts = jnp.stack([jnp.sum(d_q_norm * q_hat, axis=0), jnp.sum(d_k_norm * k_hat, axis=0)])
    d_q_hat = d_q_norm * q_gain
    d_k_hat = d_k_norm * k_gain
    dots = sum_ctx(jnp.stack([jnp.sum(d_q_hat * q_hat, axis=1), jnp.sum(d_k_hat * k_hat, axis=1)]))
    dots = dots * (1.0 / (parts * width))
    d_q_low = (qk_scale[0][:, None] * (d_q_hat - q_hat * dots[0][:, None])).astype(LOW)
    d_k_low = (qk_scale[1][:, None] * (d_k_hat - k_hat * dots[1][:, None])).astype(LOW)
    d_qkv = jnp.concatenate([d_q_low, d_k_low, d_v_low], axis=1)

    d_in_sum = scatter_ctx(dot(d_qkv, w_head, ((1,), (1,))).astype(LOW))
    d_in = swap_ws(d_in_sum.reshape(ws_count, slot_rows, width)).reshape(tokens, width)
    grad_input = d_mid + rms_back(x, x_scale, d_in.astype(HIGH) * attn_gain)

    head_grad = dot(slot_in, d_qkv, ((0,), (0,))).astype(LOW)
    head_grad = head_grad.reshape(ctx_count, ws_count, rows, 3 * HD).transpose(1, 0, 2, 3)
    head_grad = jnp.sum(swap_ws(head_grad).astype(HIGH), axis=0).astype(LOW)
    col_grad = lax.all_to_all(head_grad, "ctx", 0, 0, tiled=True).astype(HIGH)
    if parts > 1:
        col_grad = jnp.sum(col_grad.reshape(heads, parts, rows, 3 * HD), axis=1)
    grads_qkv = col_grad.reshape(heads, rows, 3, HD).transpose(2, 1, 0, 3).reshape(3, rows, width)
    own_gain = lax.dynamic_slice_in_dim(attn_gain, (c * ws_count + w) * rows, rows, 0)
    grad_attn_gain = jnp.sum(grads_qkv * own_qkv.astype(HIGH), axis=(0, 2)) / own_gain

    if parts > 1:
        gain_parts = lax.psum_scatter(
            gain_parts, "ctx", scatter_dimension=1, axis_index_groups=groups, tiled=True
        )
    gain_rows = gain_parts.reshape(2, ws_count, rows).transpose(1, 0, 2)
    grad_qk_gain = jnp.sum(swap_ws(gain_rows), axis=0)

    return (
        layer_out.reshape(1, 1, tokens, width),
        grad_input.reshape(1, 1, tokens, width),
        grad_attn_gain,
        grad_qk_gain[0],
        grad_qk_gain[1],
        grad_ffn_gain,
        grads_qkv[0],
        grads_qkv[1],
        grads_qkv[2],
        grad_w_out,
        grad_w_router,
        grad_w_gate,
        grad_w_up,
        grad_w_down,
    )


def solution(mesh):
    rows = P("ctx", "ws", None, None)
    master = P(("ctx", "ws"), None)
    expert = P("ctx", "ws", None)
    gain = P(("ctx", "ws"))
    return jax.shard_map(
        local,
        mesh=mesh,
        in_specs=(rows, rows, P(), P(), rows) + (P(),) * 4 + (master,) * 5 + (expert,) * 3,
        out_specs=(rows, rows) + (gain,) * 4 + (master,) * 5 + (expert,) * 3,
        check_vma=False,
    )
```

```python
import math

import jax
import jax.numpy as jnp
from jax import lax
from jax.experimental import pallas as pl
from jax.experimental.pallas import tpu as pltpu
from jax.sharding import PartitionSpec as P

HD = 128
SLOTS = 2

NORM_EPS = 1e-05
ROPE_BASE = 10000.0
MASK_FLOOR = -1e30

LOW = jnp.bfloat16
HIGH = jnp.float32


def dot(left, right, dims=((1,), (0,))):
    return lax.dot_general(left, right, (dims, ((), ())), preferred_element_type=HIGH)


def inv_rms(field):
    return lax.rsqrt(jnp.mean(field * field, axis=-1, keepdims=True) + NORM_EPS)


def rms_back(field, scale, d_hat):
    hat = field * scale
    return scale * (d_hat - hat * jnp.mean(d_hat * hat, axis=-1, keepdims=True))


def rope_tables(positions):
    half_dim = HD // 2
    inv_freq = jnp.exp(jnp.arange(half_dim, dtype=HIGH) * (-2.0 * math.log(ROPE_BASE) / HD))
    angles = positions.astype(HIGH)[:, None] * inv_freq[None, :]
    return jnp.cos(angles), jnp.sin(angles)


def rotate(field, cosine, sine):
    lead, tail = field[:, : HD // 2], field[:, HD // 2 :]
    return jnp.concatenate([lead * cosine - tail * sine, tail * cosine + lead * sine], axis=1)


def pair_ws(own, away):
    came = lax.ppermute(away, "ws", [(0, 1), (1, 0)])
    first = lax.axis_index("ws") == 0
    return jnp.where(first, own, came), jnp.where(first, came, own)


def swap_ws(field):
    mine = lax.axis_index("ws")
    own = lax.dynamic_index_in_dim(field, mine, 0, keepdims=False)
    away = lax.dynamic_index_in_dim(field, 1 - mine, 0, keepdims=False)
    return jnp.stack(pair_ws(own, away), axis=0)


def other_ws(field):
    return lax.ppermute(field, "ws", [(0, 1), (1, 0)])


def whole_ws(half, came):
    first = lax.axis_index("ws") == 0
    return jnp.concatenate([jnp.where(first, half, came), jnp.where(first, came, half)], axis=0)


def sum_ctx(field):
    count = lax.axis_size("ctx")
    if count & (count - 1):
        return lax.psum(field, "ctx")
    step = 1
    while step < count:
        field = field + lax.ppermute(field, "ctx", [(i, i ^ step) for i in range(count)])
        step *= 2
    return field


class Line:
    groups = 4

    def __init__(self):
        c = lax.axis_index("ctx")
        self.z, y, core = c // 4, c // 2 % 2, c % 2
        near = jnp.array([[0, 1, 2, 3], [1, 0, 2, 3], [2, 1, 3, 0], [3, 2, 1, 0]], jnp.int32)[self.z]
        flip = jnp.arange(2, dtype=jnp.int32)
        self.order = (
            near[:, None, None] * 4
            + (y ^ flip)[None, None, :] * 2
            + (core ^ flip)[None, :, None]
        ).reshape(16)
        number = jnp.arange(16, dtype=jnp.int32)
        here = self.order[None, :] == number[:, None]
        self.inverse = jnp.sum(jnp.where(here, number[None, :], 0), axis=1)

    @staticmethod
    def send(field, dz=0, dy=0, dk=0, least=0, most=3):
        pairs = []
        for c in range(16):
            z, y, core = c // 4, c // 2 % 2, c % 2
            if least <= z <= most and 0 <= z + dz <= 3:
                pairs.append((c, (z + dz) * 4 + (y ^ dy) * 2 + (core ^ dk)))
        return lax.ppermute(field, "ctx", pairs)

    def gather(self, block, fills, use):
        send, z = self.send, self.z
        bar = lax.optimization_barrier
        side0, up1, down1, filled0 = bar(
            (send(block, dy=1), send(block, 1), send(block, -1), fills[0]())
        )
        near1 = jnp.where(z == 0, down1, up1)
        pair0 = jnp.concatenate([block, side0], axis=0)
        side1, up2, down2, core0, filled1 = bar(
            (
                send(near1, dy=1),
                send(up1, 1, least=1),
                send(down1, -1, most=2),
                send(pair0, dk=1),
                fills[1](),
            )
        )
        near2 = jnp.where(z == 0, down2, jnp.where(z == 3, up2, down1))
        pair1 = jnp.concatenate([near1, side1], axis=0)
        group0 = jnp.concatenate([pair0, core0], axis=0)
        side2, up3, down3, core1, used0 = bar(
            (
                send(near2, dy=1),
                send(up2, 1, least=2),
                send(down2, -1, most=1),
                send(pair1, dk=1),
                use(0, group0),
            )
        )
        near3 = jnp.where(z == 0, down3, jnp.where(z == 1, down2, jnp.where(z == 2, up2, up3)))
        pair2 = jnp.concatenate([near2, side2], axis=0)
        group1 = jnp.concatenate([pair1, core1], axis=0)
        side3, core2, used1 = bar((send(near3, dy=1), send(pair2, dk=1), use(1, group1)))
        pair3 = jnp.concatenate([near3, side3], axis=0)
        group2 = jnp.concatenate([pair2, core2], axis=0)
        core3, used2 = bar((send(pair3, dk=1), use(2, group2)))
        group3 = jnp.concatenate([pair3, core3], axis=0)
        used3 = use(3, group3)
        return [group0, group1, group2, group3], [filled0, filled1], [used0, used1, used2, used3]

    def scatter(self, make, fills):
        send, z = self.send, self.z
        bar = lax.optimization_barrier

        def add(*fields):
            total = fields[0].astype(HIGH)
            for field in fields[1:]:
                total = total + field.astype(HIGH)
            return total.astype(LOW)

        made3 = make(3)
        rows = made3.shape[0] // 4

        def to_core(made):
            return send(made[2 * rows :], dk=1)

        def side_pair(made, core):
            both = add(made[: 2 * rows], core)
            return both[:rows], send(both[rows:], dy=1)

        core3, made2 = bar((to_core(made3), make(2)))
        own3, side3 = side_pair(made3, core3)
        side3, core2, made1 = bar((side3, to_core(made2), make(1)))
        near3 = add(own3, side3)
        own2, side2 = side_pair(made2, core2)
        up, down = send(near3, 1, most=0), send(near3, -1, least=3)
        up, down, side2, core1, made0 = bar((up, down, side2, to_core(made1), make(0)))
        near2 = add(own2, side2)
        own1, side1 = side_pair(made1, core1)
        up = send(add(jnp.where(z == 0, near2, near3), up), 1, most=1)
        down = send(add(jnp.where(z == 2, near3, near2), down), -1, least=2)
        up, down, side1, core0, filled0 = bar((up, down, side1, to_core(made0), fills[0]()))
        near1 = add(own1, side1)
        own0, side0 = side_pair(made0, core0)
        up = send(add(jnp.where(z == 0, near1, near2), up), 1)
        down = send(add(near1, down), -1)
        up, down, side0, filled1 = bar((up, down, side0, fills[1]()))
        return add(own0, side0, up, down), [filled0, filled1]

    def to_whole(self, small):
        here = self.order[None, :] == jnp.arange(16, dtype=jnp.int32)[:, None]
        return jnp.sum(jnp.where(here[:, :, None], small[None], 0), axis=1)

    def from_whole(self, small):
        here = self.order[:, None] == jnp.arange(16, dtype=jnp.int32)[None, :]
        return jnp.sum(jnp.where(here[:, :, None], small[None], 0), axis=1)

    def move(self, field, back):
        order = self.inverse if back else self.order
        rows, width = field.shape[0] // 16, field.shape[1]
        out = jax.ShapeDtypeStruct(field.shape, field.dtype)
        if width < 1024:

            def small(order_ref, in_ref, out_ref):
                for i in range(16):
                    place = pl.ds(pl.multiple_of(order_ref[i] * rows, rows), rows)
                    out_ref[i * rows : (i + 1) * rows, :] = in_ref[place, :]

            return pl.pallas_call(
                small,
                in_specs=[
                    pl.BlockSpec(memory_space=pltpu.SMEM),
                    pl.BlockSpec(memory_space=pltpu.VMEM),
                ],
                out_specs=pl.BlockSpec(memory_space=pltpu.VMEM),
                out_shape=out,
                name="move_small",
            )(order, field)

        def large(order_ref, in0, in1, in2, in3, out_ref):
            for i, in_ref in enumerate((in0, in1, in2, in3)):
                out_ref[i * rows : (i + 1) * rows, :] = in_ref[...]

        return pl.pallas_call(
            large,
            grid_spec=pltpu.PrefetchScalarGridSpec(
                num_scalar_prefetch=1,
                grid=(4,),
                in_specs=[
                    pl.BlockSpec((rows, width), lambda g, order, i=i: (order[4 * g + i], 0))
                    for i in range(4)
                ],
                out_specs=pl.BlockSpec((4 * rows, width), lambda g, order: (g, 0)),
            ),
            out_shape=out,
            compiler_params=pltpu.CompilerParams(vmem_limit_bytes=24 * 1024 * 1024),
            name="move_large",
        )(order, field, field, field, field)


class Plain:
    groups = 1

    def __init__(self):
        self.order = jnp.arange(lax.axis_size("ctx"), dtype=jnp.int32)

    def gather(self, block, fills, use):
        whole = lax.all_gather(block, "ctx", axis=0, tiled=True)
        return [whole], [fill() for fill in fills], [use(0, whole)]

    def scatter(self, make, fills):
        total = lax.psum_scatter(make(0), "ctx", scatter_dimension=0, tiled=True)
        return total, [fill() for fill in fills]

    def to_whole(self, small):
        return small

    def from_whole(self, small):
        return small

    def move(self, field, back):
        return field


def local(
    layer_input,
    out_grad,
    seq_lengths,
    block_deal,
    expert_routes,
    attn_gain,
    query_gain,
    key_gain,
    ffn_gain,
    w_query,
    w_key,
    w_value,
    w_out,
    w_router,
    w_gate,
    w_up,
    w_down,
):
    ws_count = lax.axis_size("ws")
    ctx_count = lax.axis_size("ctx")
    c = lax.axis_index("ctx")
    w = lax.axis_index("ws")
    tokens, width = layer_input.shape[2:]
    heads = width // HD
    parts = ctx_count // heads
    head = c // parts
    part = c % parts
    own_part = c // heads
    slot_rows = tokens // SLOTS
    half_block = slot_rows // 2
    rows = w_query.shape[0]
    experts = w_router.shape[1]
    span = ctx_count * tokens
    part_span = span // parts

    net = Line() if ctx_count == 16 else Plain()

    starts = block_deal.reshape(ctx_count, 1, 2, 1) * (half_block * ws_count)
    in_block = jnp.arange(half_block, dtype=jnp.int32)
    pair_pos = starts + (
        jnp.arange(ws_count, dtype=jnp.int32)[None, :, None, None] * half_block + in_block
    )
    pos_slot = net.from_whole(pair_pos.reshape(ctx_count, tokens)).reshape(span)
    live_slot = pos_slot < seq_lengths[w]
    own_pos = lax.dynamic_index_in_dim(
        (starts + w * half_block + in_block)[:, 0], c, 0, keepdims=False
    ).reshape(1, slot_rows)
    live_own = (own_pos < seq_lengths[:, None]).reshape(tokens, 1)

    x = layer_input.reshape(tokens, width).astype(HIGH)
    x_scale = inv_rms(x)
    attn_in = (x * x_scale * attn_gain).astype(LOW)
    own_qkv = jnp.stack([w_query, w_key, w_value]).astype(LOW)
    by_head = own_qkv.reshape(3, rows, heads, HD).transpose(2, 1, 0, 3).reshape(heads, rows, 3 * HD)
    if parts > 1:
        by_head = jnp.repeat(by_head, parts, axis=0)
    router_rows = jnp.broadcast_to(w_router.astype(LOW), (ctx_count, rows, experts))
    named = (
        expert_routes.reshape(tokens, 1, -1) == jnp.arange(experts, dtype=jnp.int32)[None, :, None]
    )
    named = jnp.any(named, axis=2).T.astype(LOW).reshape(ctx_count, 1, tokens)
    head_width = 3 * HD + HD * -(-experts // HD)
    sent = jnp.concatenate(
        [
            jnp.concatenate(
                [by_head, router_rows, jnp.zeros((ctx_count, rows, head_width - 3 * HD - experts), LOW)],
                axis=2,
            ),
            jnp.pad(named, ((0, 0), (0, 15), (0, head_width - tokens))),
        ],
        axis=1,
    )
    came = lax.all_to_all(sent, "ctx", 0, 0, tiled=True)
    def after(field, event):
        return lax.optimization_barrier((field, event))[0]

    own_gate, own_up, own_down = (field[0].astype(LOW) for field in (w_gate, w_up, w_down))

    def first_fill():
        return came, own_gate, own_up, own_down

    slot_own = swap_ws(attn_in.reshape(SLOTS, slot_rows, width)).reshape(tokens, width)
    state = {}

    def second_fill():
        state["gate"] = other_ws(after(own_gate, slot_own))
        return state["gate"], rope_tables(pos_slot)

    def project(g, rows_in):
        if g == 0:
            head_rows = came[None, :, :rows]
            both = whole_ws(head_rows, other_ws(after(head_rows, state["gate"])))
            state["head"] = both.transpose(1, 0, 2, 3).reshape(width, head_width)
        field = dot(rows_in, state["head"][:, : 3 * HD])
        if g == net.groups - 1:
            came_up = other_ws(after(own_up, state["head"]))
            field, state["up"] = lax.optimization_barrier((field, came_up))
        return field

    slot_groups, ((came, *_), (came_gate, (cosine, sine))), qkv = net.gather(
        slot_own, [first_fill, second_fill], project
    )
    w_head_all = state["head"]
    w_head = w_head_all[:, : 3 * HD]
    r_weight = w_head_all[:, 3 * HD : 3 * HD + experts]
    routed = net.from_whole(came[:, rows, :tokens].astype(HIGH)).reshape(span, 1) > 0.5
    came_up = state["up"]
    o_weight = lax.all_gather(after(w_out.astype(LOW), qkv[0]), ("ctx", "ws"), axis=0, tiled=True)
    grad_own = jnp.where(live_own, out_grad.reshape(tokens, width), 0).astype(LOW)
    grad_all = lax.all_gather(after(grad_own, qkv[0]), "ctx", axis=0, tiled=True)
    slot_in = jnp.concatenate(slot_groups, axis=0)
    qkv = jnp.concatenate(qkv, axis=0)

    q_pre, k_pre = qkv[:, :HD], qkv[:, HD : 2 * HD]
    v_low = qkv[:, 2 * HD :].astype(LOW)

    def sum_heads(first, second):
        both = jnp.concatenate(
            [first.reshape(ctx_count, tokens), second.reshape(ctx_count, tokens)], axis=1
        )
        both = net.from_whole(sum_ctx(net.to_whole(both))) * (1.0 / (parts * width))
        return both[:, :tokens].reshape(span, 1), both[:, tokens:].reshape(span, 1)

    q_mean, k_mean = sum_heads(jnp.sum(q_pre * q_pre, axis=1), jnp.sum(k_pre * k_pre, axis=1))
    q_scale = lax.rsqrt(q_mean + NORM_EPS)
    k_scale = lax.rsqrt(k_mean + NORM_EPS)
    q_hat = q_pre * q_scale
    k_hat = k_pre * k_scale
    q_gain = lax.dynamic_slice_in_dim(query_gain, head * HD, HD, 0)
    k_gain = lax.dynamic_slice_in_dim(key_gain, head * HD, HD, 0)
    q_low = rotate(q_hat * q_gain, cosine, sine).astype(LOW)
    k_low = rotate(k_hat * k_gain, cosine, sine).astype(LOW)

    def of_part(field):
        if parts == 1:
            return field
        return lax.dynamic_slice_in_dim(field, part * part_span, part_span, 0)

    q_part = of_part(q_low)
    pos_query = of_part(pos_slot)
    score_scale = HD ** (-0.5)
    visible = (pos_slot[None, :] <= pos_query[:, None]) & live_slot[None, :]
    scores = jnp.where(visible, dot(q_part, k_low, ((1,), (1,))) * score_scale, MASK_FLOOR)
    row_max = jnp.max(scores, axis=1, keepdims=True)
    expo = jnp.exp(scores - row_max)
    row_sum = jnp.sum(expo, axis=1, keepdims=True)
    attn_head = dot((expo / row_sum).astype(LOW), v_low)
    log_total = row_max + jnp.log(row_sum)
    attn_head_low, came_down = lax.optimization_barrier(
        (attn_head.astype(LOW), other_ws(after(own_down, came_up)))
    )

    attn_whole = net.move(attn_head_low, True)
    out_chunks = attn_whole.reshape(heads, tokens, HD)
    if parts > 1:
        out_chunks = lax.dynamic_update_slice_in_dim(
            jnp.zeros((ctx_count, tokens, HD), LOW), out_chunks, part * heads, 0
        )
    came = lax.all_to_all(out_chunks, "ctx", 0, 0, tiled=True)
    came, g_weight, u_weight = lax.optimization_barrier(
        (came, whole_ws(own_gate, came_gate), whole_ws(own_up, came_up))
    )
    if parts > 1:
        came = lax.dynamic_index_in_dim(
            came.reshape(heads, parts, tokens, HD), own_part, 1, keepdims=False
        )
    attn_rows = came.transpose(1, 0, 2).reshape(ws_count, slot_rows, width)
    attn_low = swap_ws(attn_rows).reshape(tokens, width)

    mid = x + dot(attn_low, o_weight)
    mid_scale = inv_rms(mid)
    ffn_in = (mid * mid_scale * ffn_gain).astype(LOW)
    def group(field, g):
        size = span // net.groups
        return lax.slice_in_dim(field, g * size, (g + 1) * size, axis=0)

    half = net.groups // 2

    grad_plane = net.move(grad_all, False)

    d_weight = whole_ws(own_down, came_down)
    grad_plane = after(grad_plane, ffn_in)

    def raw_first():
        return [dot(group(grad_plane, g), d_weight, ((1,), (1,))) for g in range(half)]

    def raw_second():
        return [dot(group(grad_plane, g), d_weight, ((1,), (1,))) for g in range(half, net.groups)]

    def expert(g, rows_in):
        router_prob = jax.nn.softmax(dot(rows_in, r_weight), axis=-1)
        prob_own = lax.dynamic_slice_in_dim(router_prob, c, 1, 1)
        gate = jnp.where(group(routed, g), prob_own, 0.0)
        return prob_own, gate, dot(rows_in, g_weight), dot(rows_in, u_weight)

    plane_groups, raw, forward = net.gather(ffn_in, [raw_first, raw_second], expert)
    raw = raw[0] + raw[1]
    kept = []
    for g in range(net.groups):
        prob_own, gate, gate_pre, up_pre = forward[g]
        d_hidden_raw = raw[g]
        sigma = jax.nn.sigmoid(gate_pre)
        act = gate_pre * sigma
        hidden = (act * up_pre).astype(LOW)
        d_gate = jnp.sum(hidden.astype(HIGH) * d_hidden_raw, axis=1, keepdims=True)
        d_gate = jnp.where(group(routed, g), d_gate, 0.0)
        d_hidden = gate * d_hidden_raw
        d_gate_low = (d_hidden * up_pre * (sigma * (1.0 + gate_pre * (1.0 - sigma)))).astype(LOW)
        d_up_low = (d_hidden * act).astype(LOW)
        hidden_gated = (gate * hidden.astype(HIGH)).astype(LOW)
        kept.append((prob_own, gate, hidden, hidden_gated, d_gate, d_gate_low, d_up_low))
    prob_own, gate, hidden, hidden_gated, d_gate, d_gate_low, d_up_low = (
        jnp.concatenate(fields, axis=0) for fields in zip(*kept)
    )
    plane_in = jnp.concatenate(plane_groups, axis=0)

    def grad_rows(left, right, device):
        count = left.shape[1] // ws_count
        return dot(lax.dynamic_slice_in_dim(left, device * count, count, 1), right, ((0,), (0,)))

    def away(left, right):
        return grad_rows(left, right, 1 - w).astype(LOW)

    def own(left, right, came):
        return (grad_rows(left, right, w) + came.astype(HIGH))[None]

    prob_sum = net.from_whole(sum_ctx(net.to_whole((prob_own * d_gate).reshape(ctx_count, tokens))))
    prob_sum, down_away = lax.optimization_barrier((prob_sum, away(hidden_gated, grad_plane)))
    down_came = other_ws(down_away)
    d_log = (prob_own * (d_gate - prob_sum.reshape(span, 1))).astype(LOW)
    r_column = lax.dynamic_slice_in_dim(r_weight, c, 1, 1).reshape(1, width).astype(HIGH)

    def copies_back(g):
        made = (
            dot(kept[g][5], g_weight, ((1,), (1,)))
            + dot(kept[g][6], u_weight, ((1,), (1,)))
            + group(d_log, g).astype(HIGH) * r_column
        ).astype(LOW)
        return made

    def results():
        produced = dot(hidden, d_weight).astype(LOW).astype(HIGH)
        return net.move((gate * produced).astype(LOW), True)

    d_ffn, ((gated, down_came), gate_away) = net.scatter(
        copies_back, [lambda: (results(), down_came), lambda: away(plane_in, d_gate_low)]
    )
    d_ffn = d_ffn.astype(HIGH)
    mixture = lax.psum_scatter(gated, "ctx", scatter_dimension=0, tiled=True)
    layer_out = (mid + mixture.astype(HIGH)).astype(LOW)

    router_column = jnp.sum(plane_in.astype(HIGH) * d_log.astype(HIGH), axis=0)

    mid_hat = mid * mid_scale
    ffn_gain_part = jnp.sum(d_ffn * mid_hat, axis=0)
    d_mid = grad_own.astype(HIGH) + rms_back(mid, mid_scale, d_ffn * ffn_gain)
    d_mid_low = d_mid.astype(LOW)

    d_attn = dot(d_mid_low, o_weight, ((1,), (1,))).astype(LOW)
    d_attn_rows = swap_ws(d_attn.reshape(SLOTS, slot_rows, width)).reshape(tokens, heads, HD)
    gate_came = other_ws(after(gate_away, d_attn_rows))
    in_chunks = d_attn_rows.transpose(1, 0, 2)
    if parts > 1:
        in_chunks = lax.dynamic_update_slice(
            jnp.zeros((heads, parts, tokens, HD), LOW), in_chunks[:, None], (0, own_part, 0, 0)
        ).reshape(ctx_count, tokens, HD)
    d_attn_head = lax.all_to_all(in_chunks, "ctx", 0, 0, tiled=True)
    d_attn_head, up_away = lax.optimization_barrier((d_attn_head, away(plane_in, d_up_low)))
    up_came = other_ws(up_away)
    if parts > 1:
        d_attn_head = lax.dynamic_slice_in_dim(d_attn_head, part * heads, heads, 0)
    d_attn_head = net.move(d_attn_head.reshape(part_span, HD), False)

    slot_d_mid = lax.all_gather(
        swap_ws(d_mid_low.reshape(SLOTS, slot_rows, width)).reshape(tokens, width),
        "ctx",
        axis=0,
        tiled=True,
    )
    delta = jnp.sum(d_attn_head.astype(HIGH) * attn_head, axis=1, keepdims=True)
    prob = jnp.exp(
        jnp.where(visible, dot(q_part, k_low, ((1,), (1,))) * score_scale, MASK_FLOOR) - log_total
    )
    d_prob = dot(d_attn_head, v_low, ((1,), (1,)))
    d_score = (prob * (d_prob - delta)).astype(LOW)
    d_q_part = (dot(d_score, k_low) * score_scale).astype(LOW)
    d_k_rot = (dot(d_score, q_part, ((0,), (0,))) * score_scale).astype(LOW)
    d_v_low = dot(prob.astype(LOW), d_attn_head, ((0,), (0,))).astype(LOW)
    d_q_rot = d_q_part
    if parts > 1:
        d_q_rot = lax.dynamic_update_slice_in_dim(
            jnp.zeros((span, HD), LOW), d_q_part, part * part_span, 0
        )
    d_q_norm = rotate(d_q_rot.astype(HIGH), cosine, -sine)
    d_k_norm = rotate(d_k_rot.astype(HIGH), cosine, -sine)
    gain_parts = jnp.stack([jnp.sum(d_q_norm * q_hat, axis=0), jnp.sum(d_k_norm * k_hat, axis=0)])
    d_q_hat = d_q_norm * q_gain
    d_k_hat = d_k_norm * k_gain
    q_dot, k_dot = sum_heads(jnp.sum(d_q_hat * q_hat, axis=1), jnp.sum(d_k_hat * k_hat, axis=1))
    q_dot, gate_came = lax.optimization_barrier((q_dot, gate_came))
    d_q_low = (q_scale * (d_q_hat - q_hat * q_dot)).astype(LOW)
    d_k_low = (k_scale * (d_k_hat - k_hat * k_dot)).astype(LOW)
    d_qkv = jnp.concatenate([d_q_low, d_k_low, d_v_low], axis=1)

    head_grad = dot(slot_in, d_qkv, ((0,), (0,))).astype(LOW)
    head_grad, d_qkv = lax.optimization_barrier((head_grad, d_qkv))
    head_grad = head_grad.reshape(ctx_count, ws_count, rows, 3 * HD).transpose(1, 0, 2, 3)
    head_grad = swap_ws(head_grad)

    def make_d_in(g):
        made = dot(group(d_qkv, g), w_head, ((1,), (1,))).astype(LOW)
        if g == 2:
            state["down"] = own(hidden_gated, grad_plane, down_came)
            return lax.optimization_barrier((made, state["down"]))[0]
        if g == 1:
            state["gate"] = own(plane_in, d_gate_low, gate_came)
            return lax.optimization_barrier((made, state["gate"]))[0]
        if g == 0:
            state["sum"] = jnp.sum(head_grad.astype(HIGH), axis=0).astype(LOW)
            state["up"] = own(plane_in, d_up_low, up_came)
            made, state["sum"], _ = lax.optimization_barrier((made, state["sum"], state["up"]))
        return made

    def out_grad_rows():
        out_rows = dot(attn_whole, of_part(slot_d_mid), ((0,), (0,)))
        if parts > 1:
            out_rows = lax.psum_scatter(
                out_rows, "ctx", scatter_dimension=0, axis_index_groups=groups, tiled=True
            )
        out_rows = out_rows.reshape(ws_count, rows, width)
        mine = lax.dynamic_index_in_dim(out_rows, w, 0, keepdims=False)
        sent = lax.dynamic_index_in_dim(out_rows, 1 - w, 0, keepdims=False).astype(LOW)
        return mine, sent

    groups = [[h * parts + i for i in range(parts)] for h in range(heads)]
    d_in_sum, ((out_mine, out_sent), col_grad) = net.scatter(
        make_d_in,
        [out_grad_rows, lambda: lax.all_to_all(state["sum"], "ctx", 0, 0, tiled=True)],
    )
    if net.groups == 1:
        state["down"] = own(hidden_gated, grad_plane, down_came)
        state["gate"] = own(plane_in, d_gate_low, gate_came)
    grad_w_out = out_mine + other_ws(out_sent).astype(HIGH)
    d_in = swap_ws(d_in_sum.reshape(ws_count, slot_rows, width)).reshape(tokens, width)
    grad_input = d_mid + rms_back(x, x_scale, d_in.astype(HIGH) * attn_gain)

    small = jnp.stack([ffn_gain_part, router_column]).reshape(2, ctx_count, ws_count, rows)
    small = lax.all_to_all(
        small.transpose(1, 2, 0, 3).reshape(ctx_count, 2 * ws_count * rows), "ctx", 0, 0, tiled=True
    )
    small = jnp.sum(swap_ws(after(small, col_grad).reshape(ctx_count, ws_count, 2, rows).transpose(1, 2, 0, 3)), axis=0)
    grad_ffn_gain = jnp.sum(small[0], axis=0)
    grad_w_router = small[1].T

    col_grad = col_grad.astype(HIGH)
    if parts > 1:
        col_grad = jnp.sum(col_grad.reshape(heads, parts, rows, 3 * HD), axis=1)
    grads_qkv = col_grad.reshape(heads, rows, 3, HD).transpose(2, 1, 0, 3).reshape(3, rows, width)
    own_gain = lax.dynamic_slice_in_dim(attn_gain, (c * ws_count + w) * rows, rows, 0)
    grad_attn_gain = jnp.sum(grads_qkv * own_qkv.astype(HIGH), axis=(0, 2)) / own_gain

    if parts > 1:
        gain_parts = lax.psum_scatter(
            gain_parts, "ctx", scatter_dimension=1, axis_index_groups=groups, tiled=True
        )
    gain_rows = gain_parts.reshape(2, ws_count, rows).transpose(1, 0, 2)
    grad_qk_gain = jnp.sum(swap_ws(gain_rows), axis=0)

    return (
        layer_out.reshape(1, 1, tokens, width),
        grad_input.reshape(1, 1, tokens, width),
        grad_attn_gain,
        grad_qk_gain[0],
        grad_qk_gain[1],
        grad_ffn_gain,
        grads_qkv[0],
        grads_qkv[1],
        grads_qkv[2],
        grad_w_out,
        grad_w_router,
        state["gate"],
        state["up"],
        state["down"],
    )


def solution(mesh):
    rows = P("ctx", "ws", None, None)
    master = P(("ctx", "ws"), None)
    expert = P("ctx", "ws", None)
    gain = P(("ctx", "ws"))
    return jax.shard_map(
        local,
        mesh=mesh,
        in_specs=(rows, rows, P(), P(), rows) + (P(),) * 4 + (master,) * 5 + (expert,) * 3,
        out_specs=(rows, rows) + (gain,) * 4 + (master,) * 5 + (expert,) * 3,
        check_vma=False,
    )
```

```python
import math

import jax
import jax.numpy as jnp
from jax import lax
from jax.experimental import pallas as pl
from jax.experimental.pallas import tpu as pltpu
from jax.sharding import PartitionSpec as P

HD = 128
SLOTS = 2

NORM_EPS = 1e-05
ROPE_BASE = 10000.0
MASK_FLOOR = -1e30

LOW = jnp.bfloat16
HIGH = jnp.float32


def dot(left, right, dims=((1,), (0,))):
    return lax.dot_general(left, right, (dims, ((), ())), preferred_element_type=HIGH)


def inv_rms(field):
    return lax.rsqrt(jnp.mean(field * field, axis=-1, keepdims=True) + NORM_EPS)


def rms_back(field, scale, d_hat):
    hat = field * scale
    return scale * (d_hat - hat * jnp.mean(d_hat * hat, axis=-1, keepdims=True))


def rope_tables(positions):
    half_dim = HD // 2
    inv_freq = jnp.exp(jnp.arange(half_dim, dtype=HIGH) * (-2.0 * math.log(ROPE_BASE) / HD))
    angles = positions.astype(HIGH)[:, None] * inv_freq[None, :]
    return jnp.cos(angles), jnp.sin(angles)


def rotate(field, cosine, sine):
    lead, tail = field[:, : HD // 2], field[:, HD // 2 :]
    return jnp.concatenate([lead * cosine - tail * sine, tail * cosine + lead * sine], axis=1)


def pair_ws(own, away):
    came = lax.ppermute(away, "ws", [(0, 1), (1, 0)])
    first = lax.axis_index("ws") == 0
    return jnp.where(first, own, came), jnp.where(first, came, own)


def swap_ws(field):
    mine = lax.axis_index("ws")
    own = lax.dynamic_index_in_dim(field, mine, 0, keepdims=False)
    away = lax.dynamic_index_in_dim(field, 1 - mine, 0, keepdims=False)
    return jnp.stack(pair_ws(own, away), axis=0)


def other_ws(field):
    return lax.ppermute(field, "ws", [(0, 1), (1, 0)])


def whole_ws(half, came):
    first = lax.axis_index("ws") == 0
    return jnp.concatenate([jnp.where(first, half, came), jnp.where(first, came, half)], axis=0)


def sum_ctx(field):
    count = lax.axis_size("ctx")
    if count & (count - 1):
        return lax.psum(field, "ctx")
    step = 1
    while step < count:
        field = field + lax.ppermute(field, "ctx", [(i, i ^ step) for i in range(count)])
        step *= 2
    return field


class Line:
    groups = 4

    def __init__(self):
        c = lax.axis_index("ctx")
        self.z, y, core = c // 4, c // 2 % 2, c % 2
        near = jnp.array([[0, 1, 2, 3], [1, 0, 2, 3], [2, 1, 3, 0], [3, 2, 1, 0]], jnp.int32)[self.z]
        flip = jnp.arange(2, dtype=jnp.int32)
        self.order = (
            near[:, None, None] * 4
            + (y ^ flip)[None, None, :] * 2
            + (core ^ flip)[None, :, None]
        ).reshape(16)
        number = jnp.arange(16, dtype=jnp.int32)
        here = self.order[None, :] == number[:, None]
        self.inverse = jnp.sum(jnp.where(here, number[None, :], 0), axis=1)

    @staticmethod
    def send(field, dz=0, dy=0, dk=0, least=0, most=3):
        pairs = []
        for c in range(16):
            z, y, core = c // 4, c // 2 % 2, c % 2
            if least <= z <= most and 0 <= z + dz <= 3:
                pairs.append((c, (z + dz) * 4 + (y ^ dy) * 2 + (core ^ dk)))
        return lax.ppermute(field, "ctx", pairs)

    def gather(self, block, fills, use):
        send, z = self.send, self.z
        bar = lax.optimization_barrier

        def pair(near, side):
            return jnp.concatenate([near, side], axis=0)

        side0, up1, down1, filled0 = bar(
            (send(block, dy=1), send(block, 1), send(block, -1), fills[0]())
        )
        near1 = jnp.where(z == 0, down1, up1)
        side1, up2, down2, core0, filled1 = bar(
            (
                send(near1, dy=1),
                send(up1, 1, least=1),
                send(down1, -1, most=2),
                send(pair(block, side0), dk=1),
                fills[1](),
            )
        )
        near2 = jnp.where(z == 0, down2, jnp.where(z == 3, up2, down1))
        side2, up3, down3, core1, used0 = bar(
            (
                send(near2, dy=1),
                send(up2, 1, least=2),
                send(down2, -1, most=1),
                send(pair(near1, side1), dk=1),
                use(0, (block, side0, core0)),
            )
        )
        near3 = jnp.where(z == 0, down3, jnp.where(z == 1, down2, jnp.where(z == 2, up2, up3)))
        side3, core2, used1 = bar(
            (send(near3, dy=1), send(pair(near2, side2), dk=1), use(1, (near1, side1, core1), used0))
        )
        core3, used2 = bar((send(pair(near3, side3), dk=1), use(2, (near2, side2, core2), used1)))
        used3 = use(3, (near3, side3, core3), used2)
        return [filled0, filled1], used3

    def scatter(self, make, fills):
        send, z = self.send, self.z
        bar = lax.optimization_barrier

        def add(*fields):
            total = fields[0].astype(HIGH)
            for field in fields[1:]:
                total = total + field.astype(HIGH)
            return total.astype(LOW)

        made3 = make(3)
        rows = made3.shape[0] // 4

        def to_core(made):
            return send(made[2 * rows :], dk=1)

        def side_pair(made, core):
            both = add(made[: 2 * rows], core)
            return both[:rows], send(both[rows:], dy=1)

        core3, made2 = bar((to_core(made3), make(2)))
        own3, side3 = side_pair(made3, core3)
        side3, core2, made1 = bar((side3, to_core(made2), make(1)))
        near3 = add(own3, side3)
        own2, side2 = side_pair(made2, core2)
        up, down = send(near3, 1, most=0), send(near3, -1, least=3)
        up, down, side2, core1, made0 = bar((up, down, side2, to_core(made1), make(0)))
        near2 = add(own2, side2)
        own1, side1 = side_pair(made1, core1)
        up = send(add(jnp.where(z == 0, near2, near3), up), 1, most=1)
        down = send(add(jnp.where(z == 2, near3, near2), down), -1, least=2)
        up, down, side1, core0, filled0 = bar((up, down, side1, to_core(made0), fills[0]()))
        near1 = add(own1, side1)
        own0, side0 = side_pair(made0, core0)
        up = send(add(jnp.where(z == 0, near1, near2), up), 1)
        down = send(add(near1, down), -1)
        up, down, side0, filled1 = bar((up, down, side0, fills[1]()))
        return add(own0, side0, up, down), [filled0, filled1]

    def to_whole(self, small):
        here = self.order[None, :] == jnp.arange(16, dtype=jnp.int32)[:, None]
        return jnp.sum(jnp.where(here[:, :, None], small[None], 0), axis=1)

    def from_whole(self, small):
        here = self.order[:, None] == jnp.arange(16, dtype=jnp.int32)[None, :]
        return jnp.sum(jnp.where(here[:, :, None], small[None], 0), axis=1)

    def move(self, field, back):
        order = self.inverse if back else self.order
        rows, width = field.shape[0] // 16, field.shape[1]
        out = jax.ShapeDtypeStruct(field.shape, field.dtype)
        if width < 1024:

            def small(order_ref, in_ref, out_ref):
                for i in range(16):
                    place = pl.ds(pl.multiple_of(order_ref[i] * rows, rows), rows)
                    out_ref[i * rows : (i + 1) * rows, :] = in_ref[place, :]

            return pl.pallas_call(
                small,
                in_specs=[
                    pl.BlockSpec(memory_space=pltpu.SMEM),
                    pl.BlockSpec(memory_space=pltpu.VMEM),
                ],
                out_specs=pl.BlockSpec(memory_space=pltpu.VMEM),
                out_shape=out,
                name="move_small",
            )(order, field)

        def large(order_ref, in0, in1, in2, in3, out_ref):
            for i, in_ref in enumerate((in0, in1, in2, in3)):
                out_ref[i * rows : (i + 1) * rows, :] = in_ref[...]

        return pl.pallas_call(
            large,
            grid_spec=pltpu.PrefetchScalarGridSpec(
                num_scalar_prefetch=1,
                grid=(4,),
                in_specs=[
                    pl.BlockSpec((rows, width), lambda g, order, i=i: (order[4 * g + i], 0))
                    for i in range(4)
                ],
                out_specs=pl.BlockSpec((4 * rows, width), lambda g, order: (g, 0)),
            ),
            out_shape=out,
            compiler_params=pltpu.CompilerParams(vmem_limit_bytes=24 * 1024 * 1024),
            name="move_large",
        )(order, field, field, field, field)


class Plain:
    groups = 1

    def __init__(self):
        self.order = jnp.arange(lax.axis_size("ctx"), dtype=jnp.int32)

    def gather(self, block, fills, use):
        whole = lax.all_gather(block, "ctx", axis=0, tiled=True)
        return [fill() for fill in fills], use(0, (whole,))

    def scatter(self, make, fills):
        total = lax.psum_scatter(make(0), "ctx", scatter_dimension=0, tiled=True)
        return total, [fill() for fill in fills]

    def to_whole(self, small):
        return small

    def from_whole(self, small):
        return small

    def move(self, field, back):
        return field


def kernel_params(mib):
    return pltpu.CompilerParams(vmem_limit_bytes=mib * 1024 * 1024)


def cost(matmuls, reads):
    return pl.CostEstimate(flops=2 * matmuls, bytes_accessed=reads, transcendentals=0)


def attend(q, k, v, pos_query, pos_key):
    queries, keys = q.shape[0], k.shape[0]
    block = 256 if keys <= 2048 else 128

    def body(q_ref, k_ref, v_ref, pq_ref, pk_ref, out_ref, low_ref, log_ref):
        scores = dot(q_ref[...], k_ref[...], ((1,), (1,))) * HD ** (-0.5)
        scores = jnp.where(pk_ref[...] <= pq_ref[...], scores, MASK_FLOOR)
        row_max = jnp.max(scores, axis=1, keepdims=True)
        expo = jnp.exp(scores - row_max)
        row_sum = jnp.sum(expo, axis=1, keepdims=True)
        out = dot((expo * (1.0 / row_sum)).astype(LOW), v_ref[...])
        out_ref[...] = out
        low_ref[...] = out.astype(LOW)
        log_ref[...] = row_max + jnp.log(row_sum)

    rows = pl.BlockSpec((block, HD), lambda i: (i, 0))
    whole = pl.BlockSpec((keys, HD), lambda i: (0, 0))
    column = pl.BlockSpec((block, 1), lambda i: (i, 0))
    return pl.pallas_call(
        body,
        grid=(queries // block,),
        in_specs=[rows, whole, whole, column, pl.BlockSpec((1, keys), lambda i: (0, 0))],
        out_specs=[rows, rows, column],
        out_shape=[
            jax.ShapeDtypeStruct((queries, HD), HIGH),
            jax.ShapeDtypeStruct((queries, HD), LOW),
            jax.ShapeDtypeStruct((queries, 1), HIGH),
        ],
        compiler_params=kernel_params(48),
        cost_estimate=cost(8 * queries * keys * HD, 8 * keys * HD),
        name="attend",
    )(q, k, v, pos_query.reshape(queries, 1), pos_key.reshape(1, keys))


def attend_back(q, k, v, d_out, log_total, delta, pos_query, pos_key):
    queries, keys = q.shape[0], k.shape[0]
    block = 256 if keys <= 2048 else 128
    steps = queries // block
    scale = HD ** (-0.5)

    def body(q_ref, k_ref, v_ref, do_ref, log_ref, delta_ref, pq_ref, pk_ref, dq_ref, dk_ref, dv_ref, dk_sum, dv_sum):
        step = pl.program_id(0)

        @pl.when(step == 0)
        def _():
            dk_sum[...] = jnp.zeros_like(dk_sum)
            dv_sum[...] = jnp.zeros_like(dv_sum)

        q_rows, k_rows, do_rows = q_ref[...], k_ref[...], do_ref[...]
        scores = dot(k_rows, q_rows, ((1,), (1,))) * scale
        scores = jnp.where(pk_ref[...] <= pq_ref[...], scores, MASK_FLOOR)
        prob = jnp.exp(scores - log_ref[...])
        d_prob = dot(v_ref[...], do_rows, ((1,), (1,)))
        d_score = (prob * (d_prob - delta_ref[...])).astype(LOW)
        dv_sum[...] += dot(prob.astype(LOW), do_rows)
        dk_sum[...] += dot(d_score, q_rows)
        dq_ref[...] = (dot(d_score, k_rows, ((0,), (0,))) * scale).astype(LOW)

        @pl.when(step == steps - 1)
        def _():
            dk_ref[...] = (dk_sum[...] * scale).astype(LOW)
            dv_ref[...] = dv_sum[...].astype(LOW)

    rows = pl.BlockSpec((block, HD), lambda i: (i, 0))
    whole = pl.BlockSpec((keys, HD), lambda i: (0, 0))
    row = pl.BlockSpec((1, block), lambda i: (0, i))
    column = pl.BlockSpec((keys, 1), lambda i: (0, 0))
    return pl.pallas_call(
        body,
        grid=(steps,),
        in_specs=[rows, whole, whole, rows, row, row, row, column],
        out_specs=[rows, whole, whole],
        out_shape=[
            jax.ShapeDtypeStruct((queries, HD), LOW),
            jax.ShapeDtypeStruct((keys, HD), LOW),
            jax.ShapeDtypeStruct((keys, HD), LOW),
        ],
        scratch_shapes=[pltpu.VMEM((keys, HD), HIGH), pltpu.VMEM((keys, HD), HIGH)],
        compiler_params=kernel_params(56),
        cost_estimate=cost(12 * queries * keys * HD, 8 * keys * HD),
        name="attend_back",
    )(
        q,
        k,
        v,
        d_out,
        log_total.reshape(1, queries),
        delta.reshape(1, queries),
        pos_query.reshape(1, queries),
        pos_key.reshape(keys, 1),
    )


def in_place(body, g, last, prefetch, operands, **kernel):
    outs = kernel.pop("outs")
    specs = kernel.pop("in_specs")
    count = len(operands)
    last = list(last) if last is not None else []

    def called(*refs):
        body(*refs[: prefetch + count], *refs[prefetch + count + len(last) :])

    return pl.pallas_call(
        called,
        grid_spec=pltpu.PrefetchScalarGridSpec(
            num_scalar_prefetch=prefetch,
            grid=kernel.pop("grid"),
            in_specs=specs + [pl.BlockSpec(memory_space=pl.ANY)] * len(last),
            out_specs=kernel.pop("out_specs"),
            scratch_shapes=kernel.pop("scratch_shapes", ()),
        ),
        out_shape=outs,
        input_output_aliases={prefetch + count + i: i for i in range(len(last))},
        **kernel,
    )


def fixed(rows, columns, g=0):
    return pl.BlockSpec((rows, columns), lambda j, *info: (g, 0))


def project_group(g, pieces, last, groups, w_all):
    count, width = 4 * pieces[0].shape[0], pieces[0].shape[1]
    third = count // 4

    def body(near_ref, side_ref, core_ref, w_ref, rows_ref, qk_ref, v_ref):
        rows_ref[:third, :] = near_ref[...]
        rows_ref[third : 2 * third, :] = side_ref[...]
        rows_ref[2 * third :, :] = core_ref[...]
        field = dot(rows_ref[...], w_ref[...])
        qk_ref[...] = field[:, : 2 * HD]
        v_ref[...] = field[:, 2 * HD :].astype(LOW)

    operands = [*pieces, w_all]
    return in_place(
        body,
        g,
        last,
        0,
        operands,
        grid=(1,),
        in_specs=[fixed(third, width), fixed(third, width), fixed(2 * third, width), fixed(width, 3 * HD)],
        out_specs=[fixed(count, width, g), fixed(count, 2 * HD, g), fixed(count, HD, g)],
        outs=[
            jax.ShapeDtypeStruct((groups * count, width), LOW),
            jax.ShapeDtypeStruct((groups * count, 2 * HD), HIGH),
            jax.ShapeDtypeStruct((groups * count, HD), LOW),
        ],
        compiler_params=kernel_params(58),
        cost_estimate=cost(count * width * 3 * HD, 6 * count * width),
        name="project_group",
    )(*operands, *(last or ()))


def expert_group(g, pieces, last, groups, grad_all, info, routed, g_weight, u_weight, d_weight, r_wide, experts):
    count, width = 4 * pieces[0].shape[0], pieces[0].shape[1]
    hidden_width = g_weight.shape[1]
    chunk = 256
    block = count // 4

    def body(info_ref, near_ref, side_ref, core_ref, grad0, grad1, grad2, grad3, routed_ref, wg_ref, wu_ref, wd_ref, wr_ref, rows_ref, grad_ref, hid_ref, gated_ref, dg_ref, du_ref, sum_ref, prob_ref, gate_s):
        @pl.when(pl.program_id(0) == 0)
        def _():
            rows_ref[:block, :] = near_ref[...]
            rows_ref[block : 2 * block, :] = side_ref[...]
            rows_ref[2 * block :, :] = core_ref[...]
            for i, ref in enumerate((grad0, grad1, grad2, grad3)):
                grad_ref[i * block : (i + 1) * block, :] = ref[...]
            lane = lax.broadcasted_iota(jnp.int32, (count, r_wide.shape[1]), 1)
            logits = jnp.where(lane < experts, dot(rows_ref[...], wr_ref[...]), MASK_FLOOR)
            expo = jnp.exp(logits - jnp.max(logits, axis=1, keepdims=True))
            prob = expo / jnp.sum(expo, axis=1, keepdims=True)
            own = jnp.sum(jnp.where(lane == info_ref[16], prob, 0.0), axis=1, keepdims=True)
            gate = own * routed_ref[...]
            gate_s[...] = jnp.broadcast_to(gate, gate_s.shape)
            prob_ref[...] = jnp.where(lane[:, :HD] == 0, own, gate)
            sum_ref[...] = jnp.zeros_like(sum_ref)

        rows = rows_ref[...]
        gate_pre = dot(rows, wg_ref[...])
        up_pre = dot(rows, wu_ref[...])
        raw = dot(grad_ref[...], wd_ref[...], ((1,), (1,)))
        sigma = 1.0 / (1.0 + jnp.exp(-gate_pre))
        act = gate_pre * sigma
        hidden = (act * up_pre).astype(LOW)
        wide = hidden.astype(HIGH)
        product = wide * raw
        total = product[:, :HD]
        for i in range(1, chunk // HD):
            total = total + product[:, i * HD : (i + 1) * HD]
        sum_ref[...] += total
        gate = gate_s[:, :1]
        d_hidden = gate * raw
        hid_ref[...] = hidden
        gated_ref[...] = (gate * wide).astype(LOW)
        dg_ref[...] = (d_hidden * up_pre * (sigma * (1.0 + gate_pre * (1.0 - sigma)))).astype(LOW)
        du_ref[...] = (d_hidden * act).astype(LOW)

    by_column = pl.BlockSpec((width, chunk), lambda j, info: (0, j))
    out_chunk = pl.BlockSpec((count, chunk), lambda j, info: (g, j))
    operands = [*pieces, *[grad_all] * 4, routed, g_weight, u_weight, d_weight, r_wide]
    full = groups * count
    return in_place(
        body,
        g,
        last,
        1,
        operands,
        grid=(hidden_width // chunk,),
        in_specs=[fixed(block, width), fixed(block, width), fixed(2 * block, width)]
        + [
            pl.BlockSpec((block, width), lambda j, info, i=i: (info[4 * g + i], 0))
            for i in range(4)
        ]
        + [
            fixed(count, 1, g),
            by_column,
            by_column,
            pl.BlockSpec((chunk, width), lambda j, info: (j, 0)),
            fixed(width, r_wide.shape[1]),
        ],
        out_specs=[fixed(count, width, g)] * 2 + [out_chunk] * 4 + [fixed(count, HD, g)] * 2,
        outs=[jax.ShapeDtypeStruct((full, width), LOW)] * 2
        + [jax.ShapeDtypeStruct((full, hidden_width), LOW)] * 4
        + [jax.ShapeDtypeStruct((full, HD), HIGH)] * 2,
        scratch_shapes=(pltpu.VMEM((count, HD), HIGH),),
        compiler_params=kernel_params(56),
        cost_estimate=cost(3 * count * width * hidden_width, 8 * width * hidden_width),
        name="expert_group",
    )(info, *operands, *(last or ()))


def copies_group(g, d_gate, d_up, g_weight, u_weight, d_log, r_row, groups):
    count, hidden_width = d_gate.shape[0] // groups, d_gate.shape[1]
    width = g_weight.shape[0]
    chunk = 512

    def body(dg_ref, du_ref, wg_ref, wu_ref, log_ref, r_ref, out_ref):
        made = dot(dg_ref[...], wg_ref[...], ((1,), (1,)))
        made = made + dot(du_ref[...], wu_ref[...], ((1,), (1,)))
        out_ref[...] = (made + log_ref[...] * r_ref[...]).astype(LOW)

    by_row = pl.BlockSpec((chunk, hidden_width), lambda j: (j, 0))
    return pl.pallas_call(
        body,
        grid=(width // chunk,),
        in_specs=[
            fixed(count, hidden_width, g),
            fixed(count, hidden_width, g),
            by_row,
            by_row,
            fixed(count, 1, g),
            pl.BlockSpec((1, chunk), lambda j: (0, j)),
        ],
        out_specs=pl.BlockSpec((count, chunk), lambda j: (0, j)),
        out_shape=jax.ShapeDtypeStruct((count, width), LOW),
        compiler_params=kernel_params(32),
        cost_estimate=cost(2 * count * width * hidden_width, 4 * width * hidden_width),
        name="copies_group",
    )(d_gate, d_up, g_weight, u_weight, d_log, r_row)


def local(
    layer_input,
    out_grad,
    seq_lengths,
    block_deal,
    expert_routes,
    attn_gain,
    query_gain,
    key_gain,
    ffn_gain,
    w_query,
    w_key,
    w_value,
    w_out,
    w_router,
    w_gate,
    w_up,
    w_down,
):
    ws_count = lax.axis_size("ws")
    ctx_count = lax.axis_size("ctx")
    c = lax.axis_index("ctx")
    w = lax.axis_index("ws")
    tokens, width = layer_input.shape[2:]
    heads = width // HD
    parts = ctx_count // heads
    head = c // parts
    part = c % parts
    own_part = c // heads
    slot_rows = tokens // SLOTS
    half_block = slot_rows // 2
    rows = w_query.shape[0]
    experts = w_router.shape[1]
    span = ctx_count * tokens
    part_span = span // parts

    net = Line() if ctx_count == 16 else Plain()

    starts = block_deal.reshape(ctx_count, 1, 2, 1) * (half_block * ws_count)
    in_block = jnp.arange(half_block, dtype=jnp.int32)
    pair_pos = starts + (
        jnp.arange(ws_count, dtype=jnp.int32)[None, :, None, None] * half_block + in_block
    )
    pos_slot = net.from_whole(pair_pos.reshape(ctx_count, tokens)).reshape(span)
    live_slot = pos_slot < seq_lengths[w]
    own_pos = lax.dynamic_index_in_dim(
        (starts + w * half_block + in_block)[:, 0], c, 0, keepdims=False
    ).reshape(1, slot_rows)
    live_own = (own_pos < seq_lengths[:, None]).reshape(tokens, 1)

    x = layer_input.reshape(tokens, width).astype(HIGH)
    x_scale = inv_rms(x)
    attn_in = (x * x_scale * attn_gain).astype(LOW)
    own_qkv = jnp.stack([w_query, w_key, w_value]).astype(LOW)
    by_head = own_qkv.reshape(3, rows, heads, HD).transpose(2, 1, 0, 3).reshape(heads, rows, 3 * HD)
    if parts > 1:
        by_head = jnp.repeat(by_head, parts, axis=0)
    router_rows = jnp.broadcast_to(w_router.astype(LOW), (ctx_count, rows, experts))
    named = (
        expert_routes.reshape(tokens, 1, -1) == jnp.arange(experts, dtype=jnp.int32)[None, :, None]
    )
    named = jnp.any(named, axis=2).T.astype(LOW).reshape(ctx_count, 1, tokens)
    head_width = 3 * HD + HD * -(-experts // HD)
    sent = jnp.concatenate(
        [
            jnp.concatenate(
                [by_head, router_rows, jnp.zeros((ctx_count, rows, head_width - 3 * HD - experts), LOW)],
                axis=2,
            ),
            jnp.pad(named, ((0, 0), (0, 15), (0, head_width - tokens))),
        ],
        axis=1,
    )
    came = lax.all_to_all(sent, "ctx", 0, 0, tiled=True)
    def after(field, event):
        return lax.optimization_barrier((field, event))[0]

    own_gate, own_up, own_down = (field[0].astype(LOW) for field in (w_gate, w_up, w_down))

    def first_fill():
        return came, own_gate, own_up, own_down

    slot_own = swap_ws(attn_in.reshape(SLOTS, slot_rows, width)).reshape(tokens, width)
    state = {}

    halves = [own_gate[: own_gate.shape[0] // 2], own_gate[own_gate.shape[0] // 2 :]]
    halves += [own_up[: own_up.shape[0] // 2], own_up[own_up.shape[0] // 2 :]]

    def second_fill():
        state["came"] = [other_ws(after(halves[0], slot_own))]
        return state["came"][0], rope_tables(pos_slot)

    def send_half(i, event):
        state["came"].append(other_ws(after(halves[i], event)))

    def project(g, pieces, last=None):
        if g == 0:
            head_rows = came[None, :, :rows]
            both = whole_ws(head_rows, other_ws(after(head_rows, state["came"][0])))
            state["head"] = both.transpose(1, 0, 2, 3).reshape(width, head_width)
            send_half(1, state["head"])
        if net.groups == 1:
            field = dot(pieces[0], state["head"][:, : 3 * HD])
            out = [pieces[0], field[:, : 2 * HD], field[:, 2 * HD :].astype(LOW)]
        else:
            out = list(project_group(g, pieces, last, net.groups, state["head"]))
        if g == min(1, net.groups - 1):
            out[0], state["came"][1] = lax.optimization_barrier((out[0], state["came"][1]))
            send_half(2, state["came"][1])
        if g == net.groups - 1:
            out[0], state["came"][2] = lax.optimization_barrier((out[0], state["came"][2]))
            send_half(3, state["came"][2])
        return out

    ((came, *_), (first_half, (cosine, sine))), (slot_in, qk_pre, v_low) = net.gather(
        slot_own, [first_fill, second_fill], project
    )
    w_head_all = state["head"]
    w_head = w_head_all[:, : 3 * HD]
    r_wide = w_head_all[:, 3 * HD :]
    r_weight = r_wide[:, :experts]
    routed = net.from_whole(came[:, rows, :tokens].astype(HIGH)).reshape(span, 1) > 0.5
    o_weight = lax.all_gather(after(w_out.astype(LOW), first_half), ("ctx", "ws"), axis=0, tiled=True)
    grad_own = jnp.where(live_own, out_grad.reshape(tokens, width), 0).astype(LOW)
    grad_all = lax.all_gather(after(grad_own, first_half), "ctx", axis=0, tiled=True)
    q_pre, k_pre = qk_pre[:, :HD], qk_pre[:, HD:]

    def sum_heads(first, second):
        both = jnp.concatenate(
            [first.reshape(ctx_count, tokens), second.reshape(ctx_count, tokens)], axis=1
        )
        both = net.from_whole(sum_ctx(net.to_whole(both))) * (1.0 / (parts * width))
        return both[:, :tokens].reshape(span, 1), both[:, tokens:].reshape(span, 1)

    q_mean, k_mean = sum_heads(jnp.sum(q_pre * q_pre, axis=1), jnp.sum(k_pre * k_pre, axis=1))
    q_scale = lax.rsqrt(q_mean + NORM_EPS)
    k_scale = lax.rsqrt(k_mean + NORM_EPS)
    q_hat = q_pre * q_scale
    k_hat = k_pre * k_scale
    q_gain = lax.dynamic_slice_in_dim(query_gain, head * HD, HD, 0)
    k_gain = lax.dynamic_slice_in_dim(key_gain, head * HD, HD, 0)
    q_low = rotate(q_hat * q_gain, cosine, sine).astype(LOW)
    k_low = rotate(k_hat * k_gain, cosine, sine).astype(LOW)

    def of_part(field):
        if parts == 1:
            return field
        return lax.dynamic_slice_in_dim(field, part * part_span, part_span, 0)

    q_part = of_part(q_low)
    pos_query = of_part(pos_slot)
    pos_key = jnp.where(live_slot, pos_slot, jnp.int32(2**30))
    attn_head, attn_head_low, log_total = attend(q_part, k_low, v_low, pos_query, pos_key)

    attn_whole = net.move(attn_head_low, True)
    out_chunks = attn_whole.reshape(heads, tokens, HD)
    if parts > 1:
        out_chunks = lax.dynamic_update_slice_in_dim(
            jnp.zeros((ctx_count, tokens, HD), LOW), out_chunks, part * heads, 0
        )
    came = lax.all_to_all(out_chunks, "ctx", 0, 0, tiled=True)
    came, last_half = lax.optimization_barrier((came, state["came"][3]))
    came_gate = jnp.concatenate([first_half, state["came"][1]], axis=0)
    came_up = jnp.concatenate([state["came"][2], last_half], axis=0)
    g_weight, u_weight = whole_ws(own_gate, came_gate), whole_ws(own_up, came_up)
    if parts > 1:
        came = lax.dynamic_index_in_dim(
            came.reshape(heads, parts, tokens, HD), own_part, 1, keepdims=False
        )
    attn_rows = came.transpose(1, 0, 2).reshape(ws_count, slot_rows, width)
    attn_low = swap_ws(attn_rows).reshape(tokens, width)
    half_down = own_down.shape[0] // 2
    down_first = other_ws(after(own_down[:half_down], attn_low))

    mid = x + dot(attn_low, o_weight)
    mid_scale = inv_rms(mid)
    ffn_in = (mid * mid_scale * ffn_gain).astype(LOW)
    def group(field, g):
        size = span // net.groups
        return lax.slice_in_dim(field, g * size, (g + 1) * size, axis=0)

    def expert_plain(rows_in):
        router_prob = jax.nn.softmax(dot(rows_in, r_weight), axis=-1)
        prob_own = lax.dynamic_slice_in_dim(router_prob, c, 1, 1)
        gate = jnp.where(routed, prob_own, 0.0)
        gate_pre, up_pre = dot(rows_in, g_weight), dot(rows_in, u_weight)
        raw = dot(grad_all, state["d"], ((1,), (1,)))
        sigma = jax.nn.sigmoid(gate_pre)
        act = gate_pre * sigma
        hidden = (act * up_pre).astype(LOW)
        wide = hidden.astype(HIGH)
        d_gate = jnp.where(routed, jnp.sum(wide * raw, axis=1, keepdims=True), 0.0)
        d_hidden = gate * raw
        d_gate_low = (d_hidden * up_pre * (sigma * (1.0 + gate_pre * (1.0 - sigma)))).astype(LOW)
        d_up_low = (d_hidden * act).astype(LOW)
        return prob_own, gate, hidden, (gate * wide).astype(LOW), d_gate, d_gate_low, d_up_low

    info = jnp.concatenate([net.order[:16], c.astype(jnp.int32)[None]])

    def expert(g, pieces, last=None):
        if g == 0:
            came_down = jnp.concatenate([state["first"], state["second"]], axis=0)
            state["d"] = whole_ws(own_down, after(came_down, pieces[-1]))
        if net.groups == 1:
            return (pieces[0], *expert_plain(pieces[0]))
        return expert_group(
            g,
            pieces,
            last,
            net.groups,
            grad_all,
            info,
            mask,
            g_weight,
            u_weight,
            state["d"],
            r_wide,
            experts,
        )

    mask = routed.astype(HIGH)
    def fill_first():
        state["first"] = down_first
        return down_first

    def fill_second():
        state["second"] = other_ws(after(own_down[half_down:], down_first))
        return state["second"]

    _, kept = net.gather(ffn_in, [fill_first, fill_second], expert)
    d_weight = state["d"]
    if net.groups == 1:
        plane_in, prob_own, gate, hidden, hidden_gated, d_gate, d_gate_low, d_up_low = kept
        grad_plane = grad_all
    else:
        plane_in, grad_plane, hidden, hidden_gated, d_gate_low, d_up_low, sums, prob = kept
        d_gate = mask * jnp.sum(sums, axis=1, keepdims=True)
        prob_own, gate = prob[:, :1], prob[:, 1:2]

    def grad_rows(left, right, device):
        count = left.shape[1] // ws_count
        return dot(lax.dynamic_slice_in_dim(left, device * count, count, 1), right, ((0,), (0,)))

    def away(left, right):
        return grad_rows(left, right, 1 - w).astype(LOW)

    def own(left, right, came):
        right, came = lax.optimization_barrier((right, came))
        return (grad_rows(left, right, w) + came.astype(HIGH))[None]

    prob_sum = net.from_whole(sum_ctx(net.to_whole((prob_own * d_gate).reshape(ctx_count, tokens))))
    prob_sum, down_away = lax.optimization_barrier((prob_sum, away(hidden_gated, grad_plane)))

    def cut(field):
        return field[: field.shape[0] // 2], field[field.shape[0] // 2 :]

    down_cut = cut(down_away)
    down_came = [other_ws(down_cut[0])]
    d_log = (prob_own * (d_gate - prob_sum.reshape(span, 1))).astype(LOW)
    r_column = lax.dynamic_slice_in_dim(r_weight, c, 1, 1).reshape(1, width).astype(HIGH)

    def copies_back(g):
        if net.groups > 1:
            log_column = d_log.astype(HIGH)
            made = copies_group(
                g, d_gate_low, d_up_low, g_weight, u_weight, log_column, r_column, net.groups
            )
            if g == 0:
                made, down_came[0] = lax.optimization_barrier((made, down_came[0]))
            return made
        return (
            dot(d_gate_low, g_weight, ((1,), (1,)))
            + dot(d_up_low, u_weight, ((1,), (1,)))
            + d_log.astype(HIGH) * r_column
        ).astype(LOW)

    def results():
        produced = dot(hidden, d_weight).astype(LOW).astype(HIGH)
        return net.move((gate * produced).astype(LOW), True)

    def fill_gate():
        down_came.append(other_ws(after(down_cut[1], down_came[0])))
        gate_away = away(plane_in, d_gate_low)
        return gate_away, down_came[1]

    def fill_results():
        first = other_ws(after(cut(state["gate_away"])[0], down_came[1]))
        return results(), first

    def fill_both():
        state["gate_away"], down_came[1] = lax.optimization_barrier(fill_gate())
        return down_came[1]

    d_ffn, (_, (gated, gate_first)) = net.scatter(copies_back, [fill_both, fill_results])
    down_came = jnp.concatenate(down_came, axis=0)
    d_ffn = d_ffn.astype(HIGH)


    mid_hat = mid * mid_scale
    ffn_gain_part = jnp.sum(d_ffn * mid_hat, axis=0)
    d_mid = grad_own.astype(HIGH) + rms_back(mid, mid_scale, d_ffn * ffn_gain)
    d_mid_low = d_mid.astype(LOW)

    d_attn = dot(d_mid_low, o_weight, ((1,), (1,))).astype(LOW)
    d_attn_rows = swap_ws(d_attn.reshape(SLOTS, slot_rows, width)).reshape(tokens, heads, HD)
    gate_second = other_ws(after(cut(state["gate_away"])[1], d_attn_rows))
    in_chunks = d_attn_rows.transpose(1, 0, 2)
    if parts > 1:
        in_chunks = lax.dynamic_update_slice(
            jnp.zeros((heads, parts, tokens, HD), LOW), in_chunks[:, None], (0, own_part, 0, 0)
        ).reshape(ctx_count, tokens, HD)
    d_attn_head = lax.all_to_all(in_chunks, "ctx", 0, 0, tiled=True)
    d_attn_head, gate_second, up_away = lax.optimization_barrier(
        (d_attn_head, gate_second, away(plane_in, after(d_up_low, d_attn_rows)))
    )
    gate_came = jnp.concatenate([gate_first, gate_second], axis=0)
    if parts > 1:
        d_attn_head = lax.dynamic_slice_in_dim(d_attn_head, part * heads, heads, 0)
    d_attn_head = net.move(d_attn_head.reshape(part_span, HD), False)

    slot_d_mid = lax.all_gather(
        swap_ws(d_mid_low.reshape(SLOTS, slot_rows, width)).reshape(tokens, width),
        "ctx",
        axis=0,
        tiled=True,
    )
    mixture = lax.psum_scatter(
        after(gated, slot_d_mid), "ctx", scatter_dimension=0, tiled=True
    )
    layer_out = (mid + mixture.astype(HIGH)).astype(LOW)

    delta = jnp.sum(d_attn_head.astype(HIGH) * attn_head, axis=1, keepdims=True)
    d_q_part, d_k_rot, d_v_low = attend_back(
        q_part, k_low, v_low, d_attn_head, log_total, delta, pos_query, pos_key
    )
    d_q_rot = d_q_part
    if parts > 1:
        d_q_rot = lax.dynamic_update_slice_in_dim(
            jnp.zeros((span, HD), LOW), d_q_part, part * part_span, 0
        )
    d_q_norm = rotate(d_q_rot.astype(HIGH), cosine, -sine)
    d_k_norm = rotate(d_k_rot.astype(HIGH), cosine, -sine)
    gain_parts = jnp.stack([jnp.sum(d_q_norm * q_hat, axis=0), jnp.sum(d_k_norm * k_hat, axis=0)])
    d_q_hat = d_q_norm * q_gain
    d_k_hat = d_k_norm * k_gain
    q_dot, k_dot = sum_heads(jnp.sum(d_q_hat * q_hat, axis=1), jnp.sum(d_k_hat * k_hat, axis=1))
    d_q_low = (q_scale * (d_q_hat - q_hat * q_dot)).astype(LOW)
    d_k_low = (k_scale * (d_k_hat - k_hat * k_dot)).astype(LOW)
    d_qkv = jnp.concatenate([d_q_low, d_k_low, d_v_low], axis=1)

    def head_grads():
        field = dot(slot_in, d_qkv, ((0,), (0,))).astype(LOW)
        return field.reshape(ctx_count, ws_count, rows, 3 * HD).transpose(1, 0, 2, 3)

    up_cut = cut(up_away)
    up_first = other_ws(after(up_cut[0], d_v_low))

    def make_d_in(g):
        made = dot(group(d_qkv, g), w_head, ((1,), (1,))).astype(LOW)
        if g == min(2, net.groups - 1):
            made, head_grad, state["up"] = lax.optimization_barrier((made, head_grads(), up_first))
            state["head_grad"] = swap_ws(after(head_grad, state["up"]))
        if g == min(1, net.groups - 1):
            state["down"] = own(hidden_gated, grad_plane, down_came)
            made, _ = lax.optimization_barrier((made, state["down"]))
        if g == 0:
            state["sum"] = jnp.sum(state["head_grad"].astype(HIGH), axis=0).astype(LOW)
            state["gate"] = own(plane_in, d_gate_low, gate_came)
            made, state["sum"], _ = lax.optimization_barrier((made, state["sum"], state["gate"]))
        return made

    def out_grad_rows():
        out_rows = dot(attn_whole, of_part(slot_d_mid), ((0,), (0,)))
        if parts > 1:
            out_rows = lax.psum_scatter(
                out_rows, "ctx", scatter_dimension=0, axis_index_groups=groups, tiled=True
            )
        out_rows = out_rows.reshape(ws_count, rows, width)
        mine = lax.dynamic_index_in_dim(out_rows, w, 0, keepdims=False)
        sent = lax.dynamic_index_in_dim(out_rows, 1 - w, 0, keepdims=False).astype(LOW)
        return mine, sent

    def fill_rows():
        state["up_second"] = other_ws(after(up_cut[1], state["sum"]))
        return out_grad_rows(), state["up_second"]

    def fill_up():
        came = jnp.concatenate([state["up"], state["up_second"]], axis=0)
        grad = own(plane_in, d_up_low, came)
        return lax.all_to_all(state["sum"], "ctx", 0, 0, tiled=True), grad

    groups = [[h * parts + i for i in range(parts)] for h in range(heads)]
    d_in_sum, (((out_mine, out_sent), _), (col_grad, grad_w_up)) = net.scatter(
        make_d_in,
        [fill_rows, fill_up],
    )
    grad_w_out = out_mine + other_ws(out_sent).astype(HIGH)
    d_in = swap_ws(d_in_sum.reshape(ws_count, slot_rows, width)).reshape(tokens, width)
    grad_input = d_mid + rms_back(x, x_scale, d_in.astype(HIGH) * attn_gain)

    router_column = jnp.sum(plane_in.astype(HIGH) * after(d_log, d_v_low).astype(HIGH), axis=0)
    small = jnp.stack([ffn_gain_part, router_column]).reshape(2, ctx_count, ws_count, rows)
    small = lax.all_to_all(
        small.transpose(1, 2, 0, 3).reshape(ctx_count, 2 * ws_count * rows), "ctx", 0, 0, tiled=True
    )
    small = jnp.sum(swap_ws(after(small, col_grad).reshape(ctx_count, ws_count, 2, rows).transpose(1, 2, 0, 3)), axis=0)
    grad_ffn_gain = jnp.sum(small[0], axis=0)
    grad_w_router = small[1].T

    col_grad = col_grad.astype(HIGH)
    if parts > 1:
        col_grad = jnp.sum(col_grad.reshape(heads, parts, rows, 3 * HD), axis=1)
    grads_qkv = col_grad.reshape(heads, rows, 3, HD).transpose(2, 1, 0, 3).reshape(3, rows, width)
    own_gain = lax.dynamic_slice_in_dim(attn_gain, (c * ws_count + w) * rows, rows, 0)
    grad_attn_gain = jnp.sum(grads_qkv * own_qkv.astype(HIGH), axis=(0, 2)) / own_gain

    if parts > 1:
        gain_parts = lax.psum_scatter(
            gain_parts, "ctx", scatter_dimension=1, axis_index_groups=groups, tiled=True
        )
    gain_rows = gain_parts.reshape(2, ws_count, rows).transpose(1, 0, 2)
    grad_qk_gain = jnp.sum(swap_ws(gain_rows), axis=0)

    return (
        layer_out.reshape(1, 1, tokens, width),
        grad_input.reshape(1, 1, tokens, width),
        grad_attn_gain,
        grad_qk_gain[0],
        grad_qk_gain[1],
        grad_ffn_gain,
        grads_qkv[0],
        grads_qkv[1],
        grads_qkv[2],
        grad_w_out,
        grad_w_router,
        state["gate"],
        grad_w_up,
        state["down"],
    )


def solution(mesh):
    rows = P("ctx", "ws", None, None)
    master = P(("ctx", "ws"), None)
    expert = P("ctx", "ws", None)
    gain = P(("ctx", "ws"))
    return jax.shard_map(
        local,
        mesh=mesh,
        in_specs=(rows, rows, P(), P(), rows) + (P(),) * 4 + (master,) * 5 + (expert,) * 3,
        out_specs=(rows, rows) + (gain,) * 4 + (master,) * 5 + (expert,) * 3,
        check_vma=False,
    )
```
